32 devices in a mesh: groups: 2 (over y), tensor: 4 (over z), seq: 2 (over x), dp: 2 (over core).
Axes of the slice: x: 2, y: 2, z: 4, core: 2. Of those that a mesh axis runs over, the one named last changes fastest.
Arguments:
- inputs: bfloat16 [8, 512, 8192], P(('groups', 'dp'), 'seq', 'tensor'), parts along dimension 0, may hold values from -6 to 6
- base_weight: bfloat16 [8192, 8192], P(None, 'tensor'), may hold values from -0.09375 to 0.09375
- shrink_table: bfloat16 [8, 8192, 64], P('groups', 'tensor'), parts along dimension 0, may hold values from -0.0625 to 0.0625
- expand_table: bfloat16 [8, 64, 8192], P('groups', None, 'tensor'), parts along dimension 0, may hold values from -0.75 to 0.75
- adapter_ids: int32 [8], P(('groups', 'dp')), parts along dimension 0, may hold values from 0 to 3
Outputs:
- projected: bfloat16 [8, 512, 8192], P(('groups', 'dp'), 'seq', 'tensor'), parts along dimension 0
The draws below stay inside these ranges and needn't reach their ends.
There are 2 independent parts, one for each index of `groups`. The reference program is written for one: setup_inputs(seed, part) draws one part's arguments, and reference() takes and returns one part's arrays. A program takes and returns all parts, laid end to end along the dimension named above; an argument that names none is the same for every part. Nothing has to cross between parts.
All inputs are finite; a program needn't handle non-finite values.
Results may differ from the reference program's by a relative error of at most 0.0075.
Values may be sent and summed in bfloat16 or wider, within the bound.
No kernel may reach another device: no remote copies, remote signals or barrier semaphores. Data moves between devices by JAX's collectives and lax.ppermute only.
A program may use at most 128 MiB of HBM per device.

```python
import jax
import jax.numpy as jnp
from jax import lax

D = 8192
R = 64
ADAPTERS = 4
CHATS = 4
SPAN = 512
N_TENSOR = 4


def touch_ends(result, key, smallest, top_value):
    extent = result.shape
    index_at = [jax.random.randint(jax.random.fold_in(key, axis), (), 0, extent[axis]) for axis in range(len(extent))]
    result = result.at[tuple(index_at)].set(smallest)
    longest = extent.index(max(extent))
    index_at[longest] = (index_at[longest] + 1) % extent[longest]
    return result.at[tuple(index_at)].set(top_value)


def strengthened(drawn, stream_key, source, target, parts, factor):
    def block_of(dim):
        return (jnp.arange(drawn.shape[dim]) // (drawn.shape[dim] // parts)).reshape((-1,) + (1,) * (drawn.ndim - 1 - dim))

    one_side = jax.random.permutation(stream_key, parts)[block_of(target)]
    second = (block_of(target) + parts // 2) % parts
    return jnp.where((block_of(source) == one_side) | (block_of(source) == second), factor * drawn, drawn)


def level_of(stream_key, shape, pieces, least, high):
    level, own = 1.0, jax.random.fold_in(stream_key, 6)
    for axis_at, blocks in pieces:
        draws = jnp.exp(jax.random.uniform(jax.random.fold_in(own, axis_at), (blocks,), jnp.float32, least / len(pieces), high / len(pieces)))
        level = level * jnp.repeat(draws, shape[axis_at] // blocks).reshape([-1 if axis == axis_at else 1 for axis in range(len(shape))])
    return level


def normal_values(key, extent, deviation, reach, pieces=(), kind=jnp.bfloat16):
    factor_of = level_of(key, extent, pieces, -0.22, 0.18) if pieces else 1.0
    values = jax.random.normal(key, extent, jnp.float32) * deviation * factor_of
    return jnp.minimum(jnp.maximum(values, -reach), reach).astype(kind)


def heavy_noise(own_key, dims, spread, bound, cuts, heavy, held_as=jnp.bfloat16):
    result = spread * jax.random.normal(own_key, dims, jnp.float32)
    if cuts:
        result = result * level_of(own_key, dims, cuts, -0.22, 0.18)
    return jnp.clip(strengthened(result, jax.random.fold_in(own_key, 3), *heavy), -bound, bound).astype(held_as)


def setup_inputs(seed: int = 0, part: int = 0) -> dict:
    key_list = jax.random.split(jax.random.key(seed), 6)
    part_splits = jax.random.split(jax.random.fold_in(key_list[5], part), 6)
    return {
        "inputs": normal_values(part_splits[0], (CHATS, SPAN, D), 1.0, 6.0, ((0, 2), (1, 2), (2, 4))),
        "base_weight": heavy_noise(key_list[1], (D, D), D ** -0.5, 0.09375, ((1, 4),), (0, 1, 4, 2.0)),
        "shrink_table": normal_values(part_splits[2], (ADAPTERS, D, R), D ** -0.5, 0.0625, ((1, 4),)),
        "expand_table": normal_values(part_splits[3], (ADAPTERS, R, D), R ** -0.5, 0.75, ((2, 4),)),
        "adapter_ids": touch_ends(jax.random.randint(part_splits[4], (CHATS,), 0, ADAPTERS), jax.random.fold_in(part_splits[4], 1), 0, ADAPTERS - 1).astype(jnp.int32),
    }


def reference(inputs, base_weight, shrink_table, expand_table, adapter_ids):
    width = D // N_TENSOR
    chosen_shrink = shrink_table[adapter_ids].astype(jnp.float32).reshape(CHATS, N_TENSOR, width, R)
    chosen_expand = expand_table[adapter_ids].astype(jnp.float32)
    blocks = inputs.astype(jnp.float32).reshape(CHATS, SPAN, N_TENSOR, width)
    partial_value = jnp.einsum("ctnw,cnwr->nctr", blocks, chosen_shrink)
    partial_value = lax.optimization_barrier(partial_value.astype(jnp.bfloat16))
    shrunk = jnp.sum(partial_value.astype(jnp.float32), axis=0).astype(jnp.bfloat16)
    base = jnp.dot(inputs.reshape(CHATS * SPAN, D), base_weight, preferred_element_type=jnp.float32)
    base = base.reshape(CHATS, SPAN, D)
    adapted = jnp.einsum("ctr,cre->cte", shrunk.astype(jnp.float32), chosen_expand)
    return (base + adapted).astype(jnp.bfloat16)
```

```python
import jax
import jax.numpy as jnp
from jax import lax
from jax.sharding import PartitionSpec as P

F32, BF16 = jnp.float32, jnp.bfloat16


def low_rank(inputs, shrink_table, expand_table, adapter_ids):
    chats, span, _ = inputs.shape
    rank = shrink_table.shape[-1]
    partial = jnp.concatenate(
        [
            jnp.dot(inputs[c], shrink_table[adapter_ids[c]], preferred_element_type=F32).astype(BF16)
            for c in range(chats)
        ]
    )
    every = lax.all_gather(partial.reshape(-1, 2 * rank), "tensor")
    shrunk = jnp.sum(every.astype(F32), axis=0).astype(BF16).reshape(chats, span, rank)
    return jnp.concatenate(
        [
            jnp.dot(shrunk[c], expand_table[adapter_ids[c]], preferred_element_type=F32)
            for c in range(chats)
        ]
    )


def make_local(n):
    right = [(i, (i + 1) % n) for i in range(n)]
    left = [(i, (i - 1) % n) for i in range(n)]

    def local(inputs, base_weight, shrink_table, expand_table, adapter_ids):
        chats, span, width = inputs.shape
        here = lax.axis_index("tensor")
        own = inputs.reshape(chats * span, width)

        def product(block, owner, first=0):
            rows = lax.dynamic_slice_in_dim(
                base_weight, lax.rem(owner + 2 * n, n) * width + first, block.shape[1], axis=0
            )
            return jnp.dot(block, rows, preferred_element_type=F32)

        total = low_rank(inputs, shrink_table, expand_table, adapter_ids) + product(own, here)
        from_left = from_right = own
        for step in range(1, (n - 1) // 2 + 1):
            from_left = lax.ppermute(from_left, "tensor", right)
            from_right = lax.ppermute(from_right, "tensor", left)
            total = total + product(from_left, here - step)
            total = total + product(from_right, here + step)
        if n % 2 == 0:
            half = width // 2
            one = lax.ppermute(from_left[:, :half], "tensor", right)
            two = lax.ppermute(from_right[:, half:], "tensor", left)
            total = total + product(one, here - n // 2)
            total = total + product(two, here - n // 2, half)
        return total.astype(BF16).reshape(chats, span, -1)

    return local


def solution(mesh):
    return jax.shard_map(
        make_local(mesh.shape["tensor"]),
        mesh=mesh,
        in_specs=(
            P(("groups", "dp"), "seq", "tensor"),
            P(None, "tensor"),
            P("groups", "tensor", None),
            P("groups", None, "tensor"),
            P(("groups", "dp")),
        ),
        out_specs=P(("groups", "dp"), "seq", "tensor"),
        check_vma=False,
    )
```

```python
import jax
import jax.numpy as jnp
from jax import lax
from jax.sharding import PartitionSpec as P

F32, BF16 = jnp.float32, jnp.bfloat16
PLANE = ("groups", "seq", "dp")


def shrink(inputs, shrink_table, adapter_ids):
    return jnp.concatenate(
        [
            jnp.dot(inputs[c], shrink_table[adapter_ids[c]], preferred_element_type=F32).astype(BF16)
            for c in range(inputs.shape[0])
        ]
    )


def expand(shrunk, expand_table, adapter_ids):
    chats = adapter_ids.shape[0]
    parts = shrunk.reshape(chats, -1, shrunk.shape[-1])
    return [
        jnp.dot(parts[c], expand_table[adapter_ids[c]], preferred_element_type=F32)
        for c in range(chats)
    ]


def ring(n):
    right = [(i, (i + 1) % n) for i in range(n)]
    left = [(i, (i - 1) % n) for i in range(n)]

    def local(inputs, base_weight, shrink_table, expand_table, adapter_ids):
        chats, span, width = inputs.shape
        here = lax.axis_index("tensor")
        own = inputs.reshape(chats * span, width)

        def product(block, owner, first=0):
            rows = lax.dynamic_slice_in_dim(
                base_weight, lax.rem(owner + 2 * n, n) * width + first, block.shape[1], axis=0
            )
            return jnp.dot(block, rows, preferred_element_type=F32)

        shrunk = lax.psum(shrink(inputs, shrink_table, adapter_ids), "tensor")
        total = product(own, here)
        from_left = from_right = own
        for step in range(1, (n - 1) // 2 + 1):
            from_left = lax.ppermute(from_left, "tensor", right)
            from_right = lax.ppermute(from_right, "tensor", left)
            total = total + product(from_left, here - step)
            total = total + product(from_right, here + step)
        if n > 1 and n % 2 == 0:
            half = width // 2
            one = lax.ppermute(from_left[:, :half], "tensor", right)
            two = lax.ppermute(from_right[:, half:], "tensor", left)
            total = total + product(one, here - n // 2)
            total = total + product(two, here - n // 2, half)
        total = total + jnp.concatenate(expand(shrunk, expand_table, adapter_ids))
        return total.astype(BF16).reshape(chats, span, -1)

    return local


INWARD = [(0, 1), (3, 2)]
OUTWARD = [(1, 0), (2, 3)]
ACROSS = [(1, 2), (2, 1)]
SWAP = INWARD + OUTWARD


def send(block, pairs):
    return lax.ppermute(block, "tensor", pairs)


def after(block, *earlier):
    return lax.optimization_barrier((block,) + earlier)[0]


def line(inputs, base_weight, shrink_table, expand_table, adapter_ids):
    chats, span, width = inputs.shape
    rows = chats * span
    here = lax.axis_index("tensor")
    is_end = (here == 0) | (here == 3)
    far_mid = jnp.where(here < 2, 2, 1)
    far_end = jnp.where(here < 2, 3, 0)
    own = inputs.reshape(rows, width)
    place = lax.axis_index(PLANE)
    plane = lax.axis_size(PLANE)

    chunk = rows // 4
    cuts = [slice(i * chunk, (i + 1) * chunk) for i in range(4)]

    def product(block, owner):
        part = lax.dynamic_slice_in_dim(base_weight, owner * width, width, axis=0)
        return jnp.dot(block, part, preferred_element_type=F32)

    pieces = 4
    share = 2 * width // (pieces * plane)
    lent, seen = [], []

    def inward(block):
        got = send(after(block, *seen[-2:-1]), INWARD)
        seen.append(got)
        return got

    for piece in range(pieces):
        owner = far_mid if piece < pieces // 2 else far_end
        first = owner * width + (piece % (pieces // 2)) * (2 * width // pieces) + place * share
        got = inward(lax.dynamic_slice_in_dim(base_weight, first, share, axis=0))
        lent.append(lax.all_gather(got, PLANE, tiled=True))

    mate_out = send(own, OUTWARD)
    across = send(own, ACROSS)
    mate_in = [inward(own[cut]) for cut in cuts]
    across_end = [send(block, ACROSS) for block in mate_in]
    half = 2 * chunk
    mid_out = send(across[:half], OUTWARD)
    end_out = [send(block, OUTWARD) for block in across_end[:2]]

    partial = shrink(inputs, shrink_table, adapter_ids)
    mate_partial = send(partial, SWAP)
    both = send(jnp.stack([partial, mate_partial]), ACROSS)
    shrunk = (
        partial.astype(F32) + mate_partial.astype(F32) + both[0].astype(F32) + both[1].astype(F32)
    ).astype(BF16)
    shrunk = jnp.where(is_end, send(shrunk, OUTWARD), shrunk)

    width2 = 2 * width // pieces

    def lent_product(block, which):
        return sum(
            jnp.dot(
                block[:, i * width2 : (i + 1) * width2],
                lent[which * (pieces // 2) + i],
                preferred_element_type=F32,
            )
            for i in range(pieces // 2)
        )

    made = lent_product(across[half:], 0)
    done = [
        send(
            (made[i * chunk : (i + 1) * chunk] + lent_product(across_end[2 + i], 1)).astype(BF16),
            OUTWARD,
        )
        for i in range(2)
    ]

    mate = jnp.concatenate(
        [jnp.where(is_end, mate_out[cut], got) for cut, got in zip(cuts, mate_in)]
    )
    total = product(own, here) + product(mate, here ^ 1)
    total = total + jnp.concatenate(expand(shrunk, expand_table, adapter_ids))
    first_mid = jnp.where(is_end, mid_out, across[:half])
    first_end = jnp.concatenate(
        [jnp.where(is_end, out, got) for out, got in zip(end_out, across_end[:2])]
    )
    top = total[:half] + product(first_mid, far_mid) + product(first_end, far_end)
    bottom = total[half:] + product(across[half:], far_mid)
    outs = [top.astype(BF16)]
    for i in range(2):
        part = bottom[i * chunk : (i + 1) * chunk] + product(across_end[2 + i], far_end)
        outs.append((part + done[i].astype(F32)).astype(BF16))
    return jnp.concatenate(outs).reshape(chats, span, -1)


def solution(mesh):
    n = mesh.shape["tensor"]
    return jax.shard_map(
        line if n == 4 else ring(n),
        mesh=mesh,
        in_specs=(
            P(("groups", "dp"), "seq", "tensor"),
            P(None, "tensor"),
            P("groups", "tensor", None),
            P("groups", None, "tensor"),
            P(("groups", "dp")),
        ),
        out_specs=P(("groups", "dp"), "seq", "tensor"),
        check_vma=False,
    )
```

```python
import jax
import jax.numpy as jnp
from jax import lax
from jax.sharding import PartitionSpec as P

F32, BF16 = jnp.float32, jnp.bfloat16


def shrink(inputs, shrink_table, adapter_ids):
    return jnp.concatenate(
        [
            jnp.dot(inputs[c], shrink_table[adapter_ids[c]], preferred_element_type=F32).astype(BF16)
            for c in range(inputs.shape[0])
        ]
    )


def expand(shrunk, expand_table, adapter_ids):
    chats = adapter_ids.shape[0]
    parts = shrunk.reshape(chats, -1, shrunk.shape[-1])
    return [
        jnp.dot(parts[c], expand_table[adapter_ids[c]], preferred_element_type=F32)
        for c in range(chats)
    ]


def ring(n):
    right = [(i, (i + 1) % n) for i in range(n)]
    left = [(i, (i - 1) % n) for i in range(n)]

    def local(inputs, base_weight, shrink_table, expand_table, adapter_ids):
        chats, span, width = inputs.shape
        here = lax.axis_index("tensor")
        own = inputs.reshape(chats * span, width)

        def product(block, owner, first=0):
            rows = lax.dynamic_slice_in_dim(
                base_weight, lax.rem(owner + 2 * n, n) * width + first, block.shape[1], axis=0
            )
            return jnp.dot(block, rows, preferred_element_type=F32)

        shrunk = lax.psum(shrink(inputs, shrink_table, adapter_ids), "tensor")
        total = product(own, here)
        from_left = from_right = own
        for step in range(1, (n - 1) // 2 + 1):
            from_left = lax.ppermute(from_left, "tensor", right)
            from_right = lax.ppermute(from_right, "tensor", left)
            total = total + product(from_left, here - step)
            total = total + product(from_right, here + step)
        if n > 1 and n % 2 == 0:
            half = width // 2
            one = lax.ppermute(from_left[:, :half], "tensor", right)
            two = lax.ppermute(from_right[:, half:], "tensor", left)
            total = total + product(one, here - n // 2)
            total = total + product(two, here - n // 2, half)
        total = total + jnp.concatenate(expand(shrunk, expand_table, adapter_ids))
        return total.astype(BF16).reshape(chats, span, -1)

    return local


INWARD = [(0, 1), (3, 2)]
OUTWARD = [(1, 0), (2, 3)]
ACROSS = [(1, 2), (2, 1)]


def send(block, pairs):
    return lax.ppermute(block, "tensor", pairs)


def line(inputs, base_weight, shrink_table, expand_table, adapter_ids):
    chats, span, width = inputs.shape
    rows = chats * span
    here = lax.axis_index("tensor")
    is_end = (here == 0) | (here == 3)
    far_mid = jnp.where(here < 2, 2, 1)
    far_end = jnp.where(here < 2, 3, 0)
    own = inputs.reshape(rows, width)
    half, quarter = rows // 2, rows // 4

    def product(block, owner):
        part = lax.dynamic_slice_in_dim(base_weight, owner * width, width, axis=0)
        return jnp.dot(block, part, preferred_element_type=F32)

    across_own = [send(own[:half], ACROSS), send(own[half:], ACROSS)]
    mate_out = send(own, OUTWARD)
    mate_in = send(own, INWARD)
    across_mate = [send(mate_in[:half], ACROSS), send(mate_in[half:], ACROSS)]
    mid_out = [send(block, OUTWARD) for block in across_own]
    end_out = [
        send(block, OUTWARD)
        for block in (across_mate[0], across_mate[1][:quarter], across_mate[1][quarter:])
    ]

    shrunk = lax.psum(shrink(inputs, shrink_table, adapter_ids), "tensor")
    total = product(own, here) + jnp.concatenate(expand(shrunk, expand_table, adapter_ids))
    total = total + product(jnp.where(is_end, mate_out, mate_in), here ^ 1)
    outs = []
    for i, cut in enumerate((slice(0, half), slice(half, rows))):
        part = total[cut] + product(jnp.where(is_end, mid_out[i], across_own[i]), far_mid)
        if i == 0:
            outs.append(part + product(jnp.where(is_end, end_out[0], across_mate[0]), far_end))
        else:
            for j, sub in enumerate((slice(0, quarter), slice(quarter, half))):
                block = jnp.where(is_end, end_out[1 + j], across_mate[1][sub])
                outs.append(part[sub] + product(block, far_end))
    return jnp.concatenate([o.astype(BF16) for o in outs]).reshape(chats, span, -1)


def solution(mesh):
    n = mesh.shape["tensor"]
    return jax.shard_map(
        line if n == 4 else ring(n),
        mesh=mesh,
        in_specs=(
            P(("groups", "dp"), "seq", "tensor"),
            P(None, "tensor"),
            P("groups", "tensor", None),
            P("groups", None, "tensor"),
            P(("groups", "dp")),
        ),
        out_specs=P(("groups", "dp"), "seq", "tensor"),
        check_vma=False,
    )
```

```python
import jax
import jax.numpy as jnp
from jax import lax
from jax.sharding import PartitionSpec as P

F32, BF16 = jnp.float32, jnp.bfloat16


def shrink(inputs, shrink_table, adapter_ids):
    return jnp.concatenate(
        [
            jnp.dot(inputs[c], shrink_table[adapter_ids[c]], preferred_element_type=F32).astype(BF16)
            for c in range(inputs.shape[0])
        ]
    )


def expand(shrunk, expand_table, adapter_ids):
    chats = adapter_ids.shape[0]
    parts = shrunk.reshape(chats, -1, shrunk.shape[-1])
    return [
        jnp.dot(parts[c], expand_table[adapter_ids[c]], preferred_element_type=F32)
        for c in range(chats)
    ]


def ring(n):
    right = [(i, (i + 1) % n) for i in range(n)]
    left = [(i, (i - 1) % n) for i in range(n)]

    def local(inputs, base_weight, shrink_table, expand_table, adapter_ids):
        chats, span, width = inputs.shape
        here = lax.axis_index("tensor")
        own = inputs.reshape(chats * span, width)

        def product(block, owner, first=0):
            rows = lax.dynamic_slice_in_dim(
                base_weight, lax.rem(owner + 2 * n, n) * width + first, block.shape[1], axis=0
            )
            return jnp.dot(block, rows, preferred_element_type=F32)

        shrunk = lax.psum(shrink(inputs, shrink_table, adapter_ids), "tensor")
        total = product(own, here)
        from_left = from_right = own
        for step in range(1, (n - 1) // 2 + 1):
            from_left = lax.ppermute(from_left, "tensor", right)
            from_right = lax.ppermute(from_right, "tensor", left)
            total = total + product(from_left, here - step)
            total = total + product(from_right, here + step)
        if n > 1 and n % 2 == 0:
            half = width // 2
            one = lax.ppermute(from_left[:, :half], "tensor", right)
            two = lax.ppermute(from_right[:, half:], "tensor", left)
            total = total + product(one, here - n // 2)
            total = total + product(two, here - n // 2, half)
        total = total + jnp.concatenate(expand(shrunk, expand_table, adapter_ids))
        return total.astype(BF16).reshape(chats, span, -1)

    return local


INWARD = [(0, 1), (3, 2)]
OUTWARD = [(1, 0), (2, 3)]
ACROSS = [(1, 2), (2, 1)]


def send(block, pairs):
    return lax.ppermute(block, "tensor", pairs)


def after(block, *earlier):
    return lax.optimization_barrier((block,) + earlier)[0]


def line(inputs, base_weight, shrink_table, expand_table, adapter_ids):
    chats, span, width = inputs.shape
    rows = chats * span
    here = lax.axis_index("tensor")
    is_end = (here == 0) | (here == 3)
    far_mid = jnp.where(here < 2, 2, 1)
    far_end = jnp.where(here < 2, 3, 0)
    own = inputs.reshape(rows, width)
    half, quarter = rows // 2, rows // 4

    def product(block, owner):
        part = lax.dynamic_slice_in_dim(base_weight, owner * width, width, axis=0)
        return jnp.dot(block, part, preferred_element_type=F32)

    across_own = [send(own[:half], ACROSS), send(own[half:], ACROSS)]
    mate_out = send(own, OUTWARD)
    mate_in = send(own, INWARD)
    across_mate = [send(mate_in[:half], ACROSS), send(mate_in[half:], ACROSS)]
    mid_out = [send(block, OUTWARD) for block in across_own]
    end_out = [
        send(block, OUTWARD)
        for block in (across_mate[0], across_mate[1][:quarter], across_mate[1][quarter:])
    ]

    partial = shrink(inputs, shrink_table, adapter_ids)
    shrunk = lax.psum(after(partial, across_own[0]), "tensor")
    total = product(own, here) + product(jnp.where(is_end, mate_out, mate_in), here ^ 1)
    shrunk = after(shrunk, across_mate[0])
    total = total + jnp.concatenate(expand(shrunk, expand_table, adapter_ids))
    outs = []
    for i, cut in enumerate((slice(0, half), slice(half, rows))):
        part = total[cut] + product(jnp.where(is_end, mid_out[i], across_own[i]), far_mid)
        if i == 0:
            outs.append(part + product(jnp.where(is_end, end_out[0], across_mate[0]), far_end))
        else:
            for j, sub in enumerate((slice(0, quarter), slice(quarter, half))):
                block = jnp.where(is_end, end_out[1 + j], across_mate[1][sub])
                outs.append(part[sub] + product(block, far_end))
    return jnp.concatenate([o.astype(BF16) for o in outs]).reshape(chats, span, -1)


def solution(mesh):
    n = mesh.shape["tensor"]
    return jax.shard_map(
        line if n == 4 else ring(n),
        mesh=mesh,
        in_specs=(
            P(("groups", "dp"), "seq", "tensor"),
            P(None, "tensor"),
            P("groups", "tensor", None),
            P("groups", None, "tensor"),
            P(("groups", "dp")),
        ),
        out_specs=P(("groups", "dp"), "seq", "tensor"),
        check_vma=False,
    )
```

```python
import jax
import jax.numpy as jnp
from jax import lax
from jax.sharding import PartitionSpec as P

F32, BF16 = jnp.float32, jnp.bfloat16


def shrink(inputs, shrink_table, adapter_ids):
    return jnp.concatenate(
        [
            jnp.dot(inputs[c], shrink_table[adapter_ids[c]], preferred_element_type=F32).astype(BF16)
            for c in range(inputs.shape[0])
        ]
    )


def expand(shrunk, expand_table, adapter_ids):
    chats = adapter_ids.shape[0]
    parts = shrunk.reshape(chats, -1, shrunk.shape[-1])
    return [
        jnp.dot(parts[c], expand_table[adapter_ids[c]], preferred_element_type=F32)
        for c in range(chats)
    ]


def ring(n):
    right = [(i, (i + 1) % n) for i in range(n)]
    left = [(i, (i - 1) % n) for i in range(n)]

    def local(inputs, base_weight, shrink_table, expand_table, adapter_ids):
        chats, span, width = inputs.shape
        here = lax.axis_index("tensor")
        own = inputs.reshape(chats * span, width)

        def product(block, owner, first=0):
            rows = lax.dynamic_slice_in_dim(
                base_weight, lax.rem(owner + 2 * n, n) * width + first, block.shape[1], axis=0
            )
            return jnp.dot(block, rows, preferred_element_type=F32)

        shrunk = lax.psum(shrink(inputs, shrink_table, adapter_ids), "tensor")
        total = product(own, here)
        from_left = from_right = own
        for step in range(1, (n - 1) // 2 + 1):
            from_left = lax.ppermute(from_left, "tensor", right)
            from_right = lax.ppermute(from_right, "tensor", left)
            total = total + product(from_left, here - step)
            total = total + product(from_right, here + step)
        if n > 1 and n % 2 == 0:
            half = width // 2
            one = lax.ppermute(from_left[:, :half], "tensor", right)
            two = lax.ppermute(from_right[:, half:], "tensor", left)
            total = total + product(one, here - n // 2)
            total = total + product(two, here - n // 2, half)
        total = total + jnp.concatenate(expand(shrunk, expand_table, adapter_ids))
        return total.astype(BF16).reshape(chats, span, -1)

    return local


INWARD = [(0, 1), (3, 2)]
OUTWARD = [(1, 0), (2, 3)]
ACROSS = [(1, 2), (2, 1)]
SWAP = INWARD + OUTWARD


def send(block, pairs):
    return lax.ppermute(block, "tensor", pairs)


def after(block, *earlier):
    return lax.optimization_barrier((block,) + earlier)[0]


def line(inputs, base_weight, shrink_table, expand_table, adapter_ids):
    chats, span, width = inputs.shape
    rows = chats * span
    here = lax.axis_index("tensor")
    is_end = (here == 0) | (here == 3)
    far_mid = jnp.where(here < 2, 2, 1)
    far_end = jnp.where(here < 2, 3, 0)
    own = inputs.reshape(rows, width)
    cuts = [slice(0, rows // 2), slice(rows // 2, 3 * rows // 4), slice(3 * rows // 4, rows)]

    def product(block, owner):
        part = lax.dynamic_slice_in_dim(base_weight, owner * width, width, axis=0)
        return jnp.dot(block, part, preferred_element_type=F32)

    mate_out = send(own, OUTWARD)
    mate_in = send(own, INWARD)
    across_own = send(own, ACROSS)
    partial = shrink(inputs, shrink_table, adapter_ids)
    mate_partial = send(partial, SWAP)
    total = product(own, here)

    mate_in = after(mate_in, total)
    across_mate = send(mate_in, ACROSS)
    mid_out = send(across_own, OUTWARD)
    both = send(jnp.stack([partial, mate_partial]), ACROSS)
    total = total + product(jnp.where(is_end, mate_out, mate_in), here ^ 1)

    across_mate = after(across_mate, total)
    end_out = [send(across_mate[cut], OUTWARD) for cut in cuts]
    shrunk = (
        partial.astype(F32) + mate_partial.astype(F32) + both[0].astype(F32) + both[1].astype(F32)
    ).astype(BF16)
    shrunk = jnp.where(is_end, send(shrunk, OUTWARD), shrunk)
    total = total + product(jnp.where(is_end, mid_out, across_own), far_mid)
    total = total + jnp.concatenate(expand(shrunk, expand_table, adapter_ids))
    outs = [
        total[cut] + product(jnp.where(is_end, out, across_mate[cut]), far_end)
        for cut, out in zip(cuts, end_out)
    ]
    return jnp.concatenate([o.astype(BF16) for o in outs]).reshape(chats, span, -1)


def solution(mesh):
    n = mesh.shape["tensor"]
    return jax.shard_map(
        line if n == 4 else ring(n),
        mesh=mesh,
        in_specs=(
            P(("groups", "dp"), "seq", "tensor"),
            P(None, "tensor"),
            P("groups", "tensor", None),
            P("groups", None, "tensor"),
            P(("groups", "dp")),
        ),
        out_specs=P(("groups", "dp"), "seq", "tensor"),
        check_vma=False,
    )
```

```python
import jax
import jax.numpy as jnp
from jax import lax
from jax.sharding import PartitionSpec as P

F32, BF16 = jnp.float32, jnp.bfloat16


def shrink(inputs, shrink_table, adapter_ids):
    return jnp.concatenate(
        [
            jnp.dot(inputs[c], shrink_table[adapter_ids[c]], preferred_element_type=F32).astype(BF16)
            for c in range(inputs.shape[0])
        ]
    )


def expand(shrunk, expand_table, adapter_ids):
    chats = adapter_ids.shape[0]
    parts = shrunk.reshape(chats, -1, shrunk.shape[-1])
    return [
        jnp.dot(parts[c], expand_table[adapter_ids[c]], preferred_element_type=F32)
        for c in range(chats)
    ]


def ring(n):
    right = [(i, (i + 1) % n) for i in range(n)]
    left = [(i, (i - 1) % n) for i in range(n)]

    def local(inputs, base_weight, shrink_table, expand_table, adapter_ids):
        chats, span, width = inputs.shape
        here = lax.axis_index("tensor")
        own = inputs.reshape(chats * span, width)

        def product(block, owner, first=0):
            rows = lax.dynamic_slice_in_dim(
                base_weight, lax.rem(owner + 2 * n, n) * width + first, block.shape[1], axis=0
            )
            return jnp.dot(block, rows, preferred_element_type=F32)

        shrunk = lax.psum(shrink(inputs, shrink_table, adapter_ids), "tensor")
        total = product(own, here)
        from_left = from_right = own
        for step in range(1, (n - 1) // 2 + 1):
            from_left = lax.ppermute(from_left, "tensor", right)
            from_right = lax.ppermute(from_right, "tensor", left)
            total = total + product(from_left, here - step)
            total = total + product(from_right, here + step)
        if n > 1 and n % 2 == 0:
            half = width // 2
            one = lax.ppermute(from_left[:, :half], "tensor", right)
            two = lax.ppermute(from_right[:, half:], "tensor", left)
            total = total + product(one, here - n // 2)
            total = total + product(two, here - n // 2, half)
        total = total + jnp.concatenate(expand(shrunk, expand_table, adapter_ids))
        return total.astype(BF16).reshape(chats, span, -1)

    return local


INWARD = [(0, 1), (3, 2)]
OUTWARD = [(1, 0), (2, 3)]
ACROSS = [(1, 2), (2, 1)]
SWAP = INWARD + OUTWARD


def send(block, pairs):
    return lax.ppermute(block, "tensor", pairs)


def after(block, *earlier):
    return lax.optimization_barrier((block,) + earlier)[0]


def line(inputs, base_weight, shrink_table, expand_table, adapter_ids):
    chats, span, width = inputs.shape
    rows = chats * span
    here = lax.axis_index("tensor")
    is_end = (here == 0) | (here == 3)
    far_mid = jnp.where(here < 2, 2, 1)
    far_end = jnp.where(here < 2, 3, 0)
    own = inputs.reshape(rows, width)
    half, last = width // 2, width // 8

    def product(block, owner, first=0):
        part = lax.dynamic_slice_in_dim(base_weight, owner * width + first, block.shape[1], axis=0)
        return jnp.dot(block, part, preferred_element_type=F32)

    mate_out = send(own, OUTWARD)
    mate_in = send(own, INWARD)
    mid = [send(own[:, :half], ACROSS), send(own[:, half:], ACROSS)]
    partial = shrink(inputs, shrink_table, adapter_ids)
    mate_partial = send(partial, SWAP)
    total = product(own, here)

    mid_out = [send(after(mid[0], total), OUTWARD)]
    mate_in, mate_partial = lax.optimization_barrier((mate_in, mate_partial, mid[0], total))[:2]
    both = send(jnp.stack([partial, mate_partial]), ACROSS)
    end = [send(mate_in[:, :half], ACROSS), send(mate_in[:, half:], ACROSS)]
    mid_out.append(send(mid[1], OUTWARD))
    total = total + product(jnp.where(is_end, mate_out, mate_in), here ^ 1)

    end[0], both = lax.optimization_barrier((end[0], both, total))[:2]
    end_out = [send(end[0], OUTWARD)]
    shrunk = (
        partial.astype(F32) + mate_partial.astype(F32) + both[0].astype(F32) + both[1].astype(F32)
    ).astype(BF16)
    shrunk = jnp.where(is_end, send(shrunk, OUTWARD), shrunk)
    total = total + product(jnp.where(is_end, mid_out[0], mid[0]), far_mid)

    late = after(end[1], total)
    end_out += [send(late[:, : half - last], OUTWARD), send(late[:, half - last :], OUTWARD)]
    total = total + product(jnp.where(is_end, mid_out[1], mid[1]), far_mid, half)
    total = total + jnp.concatenate(expand(shrunk, expand_table, adapter_ids))
    total = total + product(jnp.where(is_end, end_out[0], end[0]), far_end)
    block = jnp.where(is_end, after(end_out[1], total), late[:, : half - last])
    total = total + product(block, far_end, half)
    block = jnp.where(is_end, after(end_out[2], total), late[:, half - last :])
    total = total + product(block, far_end, width - last)
    return total.astype(BF16).reshape(chats, span, -1)


def solution(mesh):
    n = mesh.shape["tensor"]
    return jax.shard_map(
        line if n == 4 else ring(n),
        mesh=mesh,
        in_specs=(
            P(("groups", "dp"), "seq", "tensor"),
            P(None, "tensor"),
            P("groups", "tensor", None),
            P("groups", None, "tensor"),
            P(("groups", "dp")),
        ),
        out_specs=P(("groups", "dp"), "seq", "tensor"),
        check_vma=False,
    )
```

```python
import jax
import jax.numpy as jnp
from jax import lax
from jax.sharding import PartitionSpec as P

F32, BF16 = jnp.float32, jnp.bfloat16


def shrink(inputs, shrink_table, adapter_ids):
    return jnp.concatenate(
        [
            jnp.dot(inputs[c], shrink_table[adapter_ids[c]], preferred_element_type=F32).astype(BF16)
            for c in range(inputs.shape[0])
        ]
    )


def expand(shrunk, expand_table, adapter_ids):
    chats = adapter_ids.shape[0]
    parts = shrunk.reshape(chats, -1, shrunk.shape[-1])
    return [
        jnp.dot(parts[c], expand_table[adapter_ids[c]], preferred_element_type=F32)
        for c in range(chats)
    ]


def ring(n):
    right = [(i, (i + 1) % n) for i in range(n)]
    left = [(i, (i - 1) % n) for i in range(n)]

    def local(inputs, base_weight, shrink_table, expand_table, adapter_ids):
        chats, span, width = inputs.shape
        here = lax.axis_index("tensor")
        own = inputs.reshape(chats * span, width)

        def product(block, owner, first=0):
            rows = lax.dynamic_slice_in_dim(
                base_weight, lax.rem(owner + 2 * n, n) * width + first, block.shape[1], axis=0
            )
            return jnp.dot(block, rows, preferred_element_type=F32)

        shrunk = lax.psum(shrink(inputs, shrink_table, adapter_ids), "tensor")
        total = product(own, here)
        from_left = from_right = own
        for step in range(1, (n - 1) // 2 + 1):
            from_left = lax.ppermute(from_left, "tensor", right)
            from_right = lax.ppermute(from_right, "tensor", left)
            total = total + product(from_left, here - step)
            total = total + product(from_right, here + step)
        if n > 1 and n % 2 == 0:
            half = width // 2
            one = lax.ppermute(from_left[:, :half], "tensor", right)
            two = lax.ppermute(from_right[:, half:], "tensor", left)
            total = total + product(one, here - n // 2)
            total = total + product(two, here - n // 2, half)
        total = total + jnp.concatenate(expand(shrunk, expand_table, adapter_ids))
        return total.astype(BF16).reshape(chats, span, -1)

    return local


INWARD = [(0, 1), (3, 2)]
OUTWARD = [(1, 0), (2, 3)]
ACROSS = [(1, 2), (2, 1)]
SWAP = INWARD + OUTWARD


def send(block, pairs):
    return lax.ppermute(block, "tensor", pairs)


def after(block, *earlier):
    return lax.optimization_barrier((block,) + earlier)[0]


def line(inputs, base_weight, shrink_table, expand_table, adapter_ids):
    chats, span, width = inputs.shape
    rows = chats * span
    here = lax.axis_index("tensor")
    is_end = (here == 0) | (here == 3)
    far_mid = jnp.where(here < 2, 2, 1)
    far_end = jnp.where(here < 2, 3, 0)
    own = inputs.reshape(rows, width)
    half, last = width // 2, width // 8

    def product(block, owner, first=0):
        part = lax.dynamic_slice_in_dim(base_weight, owner * width + first, block.shape[1], axis=0)
        return jnp.dot(block, part, preferred_element_type=F32)

    mate_out = send(own, OUTWARD)
    mate_in = send(own, INWARD)
    mid = [send(own[:, :half], ACROSS)]
    mid.append(send(after(own[:, half:], mid[0]), ACROSS))
    partial = shrink(inputs, shrink_table, adapter_ids)
    mate_partial = send(partial, SWAP)
    total = product(own, here)

    mid_out = [send(after(mid[0], total), OUTWARD)]
    mate_in, mate_partial = lax.optimization_barrier((mate_in, mate_partial, mid[1], total))[:2]
    both = send(jnp.stack([partial, mate_partial]), ACROSS)
    end = [send(mate_in[:, :half], ACROSS)]
    end.append(send(after(mate_in[:, half:], end[0]), ACROSS))
    mid_out.append(send(mid[1], OUTWARD))
    total = total + product(jnp.where(is_end, mate_out, mate_in), here ^ 1)

    end[0], both = lax.optimization_barrier((end[0], both, total))[:2]
    end_out = [send(end[0], OUTWARD)]
    shrunk = (
        partial.astype(F32) + mate_partial.astype(F32) + both[0].astype(F32) + both[1].astype(F32)
    ).astype(BF16)
    shrunk = jnp.where(is_end, send(shrunk, OUTWARD), shrunk)
    total = total + product(jnp.where(is_end, mid_out[0], mid[0]), far_mid)

    late = after(end[1], total)
    shrunk = after(shrunk, late)
    end_out += [send(late[:, : half - last], OUTWARD), send(late[:, half - last :], OUTWARD)]
    total = total + product(jnp.where(is_end, mid_out[1], mid[1]), far_mid, half)
    total = total + jnp.concatenate(expand(shrunk, expand_table, adapter_ids))
    total = total + product(jnp.where(is_end, end_out[0], end[0]), far_end)
    block = jnp.where(is_end, after(end_out[1], total), late[:, : half - last])
    total = total + product(block, far_end, half)
    block = jnp.where(is_end, after(end_out[2], total), late[:, half - last :])
    total = total + product(block, far_end, width - last)
    return total.astype(BF16).reshape(chats, span, -1)


def solution(mesh):
    n = mesh.shape["tensor"]
    return jax.shard_map(
        line if n == 4 else ring(n),
        mesh=mesh,
        in_specs=(
            P(("groups", "dp"), "seq", "tensor"),
            P(None, "tensor"),
            P("groups", "tensor", None),
            P("groups", None, "tensor"),
            P(("groups", "dp")),
        ),
        out_specs=P(("groups", "dp"), "seq", "tensor"),
        check_vma=False,
    )
```

```python
import jax
import jax.numpy as jnp
from jax import lax
from jax.sharding import PartitionSpec as P

F32, BF16 = jnp.float32, jnp.bfloat16


def shrink(inputs, shrink_table, adapter_ids):
    return jnp.concatenate(
        [
            jnp.dot(inputs[c], shrink_table[adapter_ids[c]], preferred_element_type=F32).astype(BF16)
            for c in range(inputs.shape[0])
        ]
    )


def expand(shrunk, expand_table, adapter_ids):
    chats = adapter_ids.shape[0]
    parts = shrunk.reshape(chats, -1, shrunk.shape[-1])
    return [
        jnp.dot(parts[c], expand_table[adapter_ids[c]], preferred_element_type=F32)
        for c in range(chats)
    ]


def ring(n):
    right = [(i, (i + 1) % n) for i in range(n)]
    left = [(i, (i - 1) % n) for i in range(n)]

    def local(inputs, base_weight, shrink_table, expand_table, adapter_ids):
        chats, span, width = inputs.shape
        here = lax.axis_index("tensor")
        own = inputs.reshape(chats * span, width)

        def product(block, owner, first=0):
            rows = lax.dynamic_slice_in_dim(
                base_weight, lax.rem(owner + 2 * n, n) * width + first, block.shape[1], axis=0
            )
            return jnp.dot(block, rows, preferred_element_type=F32)

        shrunk = lax.psum(shrink(inputs, shrink_table, adapter_ids), "tensor")
        total = product(own, here)
        from_left = from_right = own
        for step in range(1, (n - 1) // 2 + 1):
            from_left = lax.ppermute(from_left, "tensor", right)
            from_right = lax.ppermute(from_right, "tensor", left)
            total = total + product(from_left, here - step)
            total = total + product(from_right, here + step)
        if n > 1 and n % 2 == 0:
            half = width // 2
            one = lax.ppermute(from_left[:, :half], "tensor", right)
            two = lax.ppermute(from_right[:, half:], "tensor", left)
            total = total + product(one, here - n // 2)
            total = total + product(two, here - n // 2, half)
        total = total + jnp.concatenate(expand(shrunk, expand_table, adapter_ids))
        return total.astype(BF16).reshape(chats, span, -1)

    return local


INWARD = [(0, 1), (3, 2)]
OUTWARD = [(1, 0), (2, 3)]
ACROSS = [(1, 2), (2, 1)]
SWAP = INWARD + OUTWARD


def send(block, pairs):
    return lax.ppermute(block, "tensor", pairs)


def after(block, *earlier):
    return lax.optimization_barrier((block,) + earlier)[0]


def line(inputs, base_weight, shrink_table, expand_table, adapter_ids):
    chats, span, width = inputs.shape
    rows = chats * span
    here = lax.axis_index("tensor")
    is_end = (here == 0) | (here == 3)
    far_mid = jnp.where(here < 2, 2, 1)
    far_end = jnp.where(here < 2, 3, 0)
    own = inputs.reshape(rows, width)
    half, last = width // 2, width // 8

    def product(block, owner, first=0):
        part = lax.dynamic_slice_in_dim(base_weight, owner * width + first, block.shape[1], axis=0)
        return jnp.dot(block, part, preferred_element_type=F32)

    mid = send(own, ACROSS)
    mate_out = send(own, OUTWARD)
    mate_in = send(own, INWARD)
    partial = shrink(inputs, shrink_table, adapter_ids)
    mate_partial = send(partial, SWAP)
    total = product(own, here)

    mid = after(mid, total)
    mid_out = send(mid, OUTWARD)
    mate_in, mate_out, mate_partial = lax.optimization_barrier(
        (mate_in, mate_out, mate_partial, mid)
    )[:3]
    both = send(jnp.stack([partial, mate_partial]), ACROSS)
    end = [send(mate_in[:, :half], ACROSS)]
    end.append(send(after(mate_in[:, half:], end[0]), ACROSS))
    total = total + product(jnp.where(is_end, mate_out, mate_in), here ^ 1)

    end[0], both = lax.optimization_barrier((end[0], both, total))[:2]
    end_out = [send(end[0], OUTWARD)]
    shrunk = (
        partial.astype(F32) + mate_partial.astype(F32) + both[0].astype(F32) + both[1].astype(F32)
    ).astype(BF16)
    shrunk = jnp.where(is_end, send(shrunk, OUTWARD), shrunk)

    late = after(end[1], end[0])
    end_out += [send(late[:, : half - last], OUTWARD), send(late[:, half - last :], OUTWARD)]
    mid_out, shrunk = lax.optimization_barrier((mid_out, shrunk, late))[:2]
    total = total + product(jnp.where(is_end, mid_out, mid), far_mid)
    total = total + jnp.concatenate(expand(shrunk, expand_table, adapter_ids))
    total = total + product(jnp.where(is_end, after(end_out[0], total), end[0]), far_end)
    block = jnp.where(is_end, after(end_out[1], total), late[:, : half - last])
    total = total + product(block, far_end, half)
    block = jnp.where(is_end, after(end_out[2], total), late[:, half - last :])
    total = total + product(block, far_end, width - last)
    return total.astype(BF16).reshape(chats, span, -1)


def solution(mesh):
    n = mesh.shape["tensor"]
    return jax.shard_map(
        line if n == 4 else ring(n),
        mesh=mesh,
        in_specs=(
            P(("groups", "dp"), "seq", "tensor"),
            P(None, "tensor"),
            P("groups", "tensor", None),
            P("groups", None, "tensor"),
            P(("groups", "dp")),
        ),
        out_specs=P(("groups", "dp"), "seq", "tensor"),
        check_vma=False,
    )
```

```python
import jax
import jax.numpy as jnp
from jax import lax
from jax.sharding import PartitionSpec as P

F32, BF16 = jnp.float32, jnp.bfloat16


def shrink(inputs, shrink_table, adapter_ids):
    return jnp.concatenate(
        [
            jnp.dot(inputs[c], shrink_table[adapter_ids[c]], preferred_element_type=F32).astype(BF16)
            for c in range(inputs.shape[0])
        ]
    )


def expand(shrunk, expand_table, adapter_ids):
    chats = adapter_ids.shape[0]
    parts = shrunk.reshape(chats, -1, shrunk.shape[-1])
    return [
        jnp.dot(parts[c], expand_table[adapter_ids[c]], preferred_element_type=F32)
        for c in range(chats)
    ]


def ring(n):
    right = [(i, (i + 1) % n) for i in range(n)]
    left = [(i, (i - 1) % n) for i in range(n)]

    def local(inputs, base_weight, shrink_table, expand_table, adapter_ids):
        chats, span, width = inputs.shape
        here = lax.axis_index("tensor")
        own = inputs.reshape(chats * span, width)

        def product(block, owner, first=0):
            rows = lax.dynamic_slice_in_dim(
                base_weight, lax.rem(owner + 2 * n, n) * width + first, block.shape[1], axis=0
            )
            return jnp.dot(block, rows, preferred_element_type=F32)

        shrunk = lax.psum(shrink(inputs, shrink_table, adapter_ids), "tensor")
        total = product(own, here)
        from_left = from_right = own
        for step in range(1, (n - 1) // 2 + 1):
            from_left = lax.ppermute(from_left, "tensor", right)
            from_right = lax.ppermute(from_right, "tensor", left)
            total = total + product(from_left, here - step)
            total = total + product(from_right, here + step)
        if n > 1 and n % 2 == 0:
            half = width // 2
            one = lax.ppermute(from_left[:, :half], "tensor", right)
            two = lax.ppermute(from_right[:, half:], "tensor", left)
            total = total + product(one, here - n // 2)
            total = total + product(two, here - n // 2, half)
        total = total + jnp.concatenate(expand(shrunk, expand_table, adapter_ids))
        return total.astype(BF16).reshape(chats, span, -1)

    return local


INWARD = [(0, 1), (3, 2)]
OUTWARD = [(1, 0), (2, 3)]
ACROSS = [(1, 2), (2, 1)]


def send(block, pairs):
    return lax.ppermute(block, "tensor", pairs)


def after(block, *earlier):
    return lax.optimization_barrier((block,) + earlier)[0]


def line(inputs, base_weight, shrink_table, expand_table, adapter_ids):
    chats, span, width = inputs.shape
    rows = chats * span
    here = lax.axis_index("tensor")
    is_end = (here == 0) | (here == 3)
    far_mid = jnp.where(here < 2, 2, 1)
    far_end = jnp.where(here < 2, 3, 0)
    own = inputs.reshape(rows, width)
    half, last = width // 2, width // 8

    def product(block, owner, first=0):
        part = lax.dynamic_slice_in_dim(base_weight, owner * width + first, block.shape[1], axis=0)
        return jnp.dot(block, part, preferred_element_type=F32)

    mate_out = send(own, OUTWARD)
    mate_in = send(own, INWARD)
    mid = [send(own[:, :half], ACROSS)]
    partial = shrink(inputs, shrink_table, adapter_ids)
    mid.append(send(after(own, partial)[:, half:], ACROSS))
    mate_partial = send(partial, INWARD)
    total = product(own, here)

    mid_out = [send(after(mid[0], total), OUTWARD)]
    mate_in, mate_partial = lax.optimization_barrier((mate_in, mate_partial, mid[1], total))[:2]
    both = send(jnp.stack([partial, mate_partial]), ACROSS)
    end = [send(mate_in[:, :half], ACROSS)]
    end.append(send(after(mate_in, end[0])[:, half:], ACROSS))
    mid_out.append(send(mid[1], OUTWARD))
    total = total + product(jnp.where(is_end, mate_out, mate_in), here ^ 1)

    end[0], both = lax.optimization_barrier((end[0], both, total))[:2]
    end_out = [send(end[0], OUTWARD)]
    shrunk = (
        partial.astype(F32) + mate_partial.astype(F32) + both[0].astype(F32) + both[1].astype(F32)
    ).astype(BF16)
    shrunk = jnp.where(is_end, send(shrunk, OUTWARD), shrunk)
    total = total + product(jnp.where(is_end, mid_out[0], mid[0]), far_mid)

    late = after(end[1], total)
    shrunk = after(shrunk, late)
    end_out += [send(late[:, : half - last], OUTWARD), send(late[:, half - last :], OUTWARD)]
    total = total + product(jnp.where(is_end, mid_out[1], mid[1]), far_mid, half)
    total = total + jnp.concatenate(expand(shrunk, expand_table, adapter_ids))
    total = total + product(jnp.where(is_end, end_out[0], end[0]), far_end)
    block = jnp.where(is_end, after(end_out[1], total), late[:, : half - last])
    total = total + product(block, far_end, half)
    block = jnp.where(is_end, after(end_out[2], total), late[:, half - last :])
    total = total + product(block, far_end, width - last)
    return total.astype(BF16).reshape(chats, span, -1)


def solution(mesh):
    n = mesh.shape["tensor"]
    return jax.shard_map(
        line if n == 4 else ring(n),
        mesh=mesh,
        in_specs=(
            P(("groups", "dp"), "seq", "tensor"),
            P(None, "tensor"),
            P("groups", "tensor", None),
            P("groups", None, "tensor"),
            P(("groups", "dp")),
        ),
        out_specs=P(("groups", "dp"), "seq", "tensor"),
        check_vma=False,
    )
```

```python
import jax
import jax.numpy as jnp
from jax import lax
from jax.sharding import PartitionSpec as P

F32, BF16 = jnp.float32, jnp.bfloat16


def shrink(inputs, shrink_table, adapter_ids):
    return jnp.concatenate(
        [
            jnp.dot(inputs[c], shrink_table[adapter_ids[c]], preferred_element_type=F32).astype(BF16)
            for c in range(inputs.shape[0])
        ]
    )


def expand(shrunk, expand_table, adapter_ids):
    chats = adapter_ids.shape[0]
    parts = shrunk.reshape(chats, -1, shrunk.shape[-1])
    return [
        jnp.dot(parts[c], expand_table[adapter_ids[c]], preferred_element_type=F32)
        for c in range(chats)
    ]


def ring(n):
    right = [(i, (i + 1) % n) for i in range(n)]
    left = [(i, (i - 1) % n) for i in range(n)]

    def local(inputs, base_weight, shrink_table, expand_table, adapter_ids):
        chats, span, width = inputs.shape
        here = lax.axis_index("tensor")
        own = inputs.reshape(chats * span, width)

        def product(block, owner, first=0):
            rows = lax.dynamic_slice_in_dim(
                base_weight, lax.rem(owner + 2 * n, n) * width + first, block.shape[1], axis=0
            )
            return jnp.dot(block, rows, preferred_element_type=F32)

        shrunk = lax.psum(shrink(inputs, shrink_table, adapter_ids), "tensor")
        total = product(own, here)
        from_left = from_right = own
        for step in range(1, (n - 1) // 2 + 1):
            from_left = lax.ppermute(from_left, "tensor", right)
            from_right = lax.ppermute(from_right, "tensor", left)
            total = total + product(from_left, here - step)
            total = total + product(from_right, here + step)
        if n > 1 and n % 2 == 0:
            half = width // 2
            one = lax.ppermute(from_left[:, :half], "tensor", right)
            two = lax.ppermute(from_right[:, half:], "tensor", left)
            total = total + product(one, here - n // 2)
            total = total + product(two, here - n // 2, half)
        total = total + jnp.concatenate(expand(shrunk, expand_table, adapter_ids))
        return total.astype(BF16).reshape(chats, span, -1)

    return local


INWARD = [(0, 1), (3, 2)]
OUTWARD = [(1, 0), (2, 3)]
ACROSS = [(1, 2), (2, 1)]


def send(block, pairs):
    return lax.ppermute(block, "tensor", pairs)


def after(block, *earlier):
    return lax.optimization_barrier((block,) + earlier)[0]


def line(inputs, base_weight, shrink_table, expand_table, adapter_ids):
    chats, span, width = inputs.shape
    rows = chats * span
    here = lax.axis_index("tensor")
    is_end = (here == 0) | (here == 3)
    far_mid = jnp.where(here < 2, 2, 1)
    far_end = jnp.where(here < 2, 3, 0)
    own = inputs.reshape(rows, width)
    half, last = width // 2, width // 16

    def product(block, owner, first=0):
        part = lax.dynamic_slice_in_dim(base_weight, owner * width + first, block.shape[1], axis=0)
        return jnp.dot(block, part, preferred_element_type=F32)

    mate_in = send(own, INWARD)
    mate_out = send(own, OUTWARD)
    mid = [send(own[:, :half], ACROSS)]
    partial = shrink(inputs, shrink_table, adapter_ids)
    mid.append(send(after(own, partial)[:, half:], ACROSS))
    mate_partial = send(partial, INWARD)
    total = product(own, here)

    mid_out = [send(after(mid[0], total), OUTWARD)]
    mate_in, mate_out, mate_partial = lax.optimization_barrier(
        (mate_in, mate_out, mate_partial, mid[1], total)
    )[:3]
    both = send(jnp.stack([partial, mate_partial]), ACROSS)
    end = [send(mate_in[:, :half], ACROSS)]
    end.append(send(after(mate_in, end[0])[:, half:], ACROSS))
    mid_out.append(send(mid[1], OUTWARD))
    total = total + product(jnp.where(is_end, mate_out, mate_in), here ^ 1)

    end[0], both = lax.optimization_barrier((end[0], both, total))[:2]
    end_out = [send(end[0], OUTWARD)]
    shrunk = (
        partial.astype(F32) + mate_partial.astype(F32) + both[0].astype(F32) + both[1].astype(F32)
    ).astype(BF16)
    shrunk = jnp.where(is_end, send(shrunk, OUTWARD), shrunk)
    total = total + product(jnp.where(is_end, mid_out[0], mid[0]), far_mid)

    late = after(end[1], total)
    shrunk = after(shrunk, late)
    end_out += [send(late[:, : half - last], OUTWARD), send(late[:, half - last :], OUTWARD)]
    total = total + product(jnp.where(is_end, mid_out[1], mid[1]), far_mid, half)
    total = total + jnp.concatenate(expand(shrunk, expand_table, adapter_ids))
    total = total + product(jnp.where(is_end, end_out[0], end[0]), far_end)
    block = jnp.where(is_end, after(end_out[1], total), late[:, : half - last])
    total = total + product(block, far_end, half)
    block = jnp.where(is_end, after(end_out[2], total), late[:, half - last :])
    total = total + product(block, far_end, width - last)
    return total.astype(BF16).reshape(chats, span, -1)


def solution(mesh):
    n = mesh.shape["tensor"]
    return jax.shard_map(
        line if n == 4 else ring(n),
        mesh=mesh,
        in_specs=(
            P(("groups", "dp"), "seq", "tensor"),
            P(None, "tensor"),
            P("groups", "tensor", None),
            P("groups", None, "tensor"),
            P(("groups", "dp")),
        ),
        out_specs=P(("groups", "dp"), "seq", "tensor"),
        check_vma=False,
    )
```

```python
import jax
import jax.numpy as jnp
from jax import lax
from jax.sharding import PartitionSpec as P

F32, BF16 = jnp.float32, jnp.bfloat16


def shrink(inputs, shrink_table, adapter_ids):
    return jnp.concatenate(
        [
            jnp.dot(inputs[c], shrink_table[adapter_ids[c]], preferred_element_type=F32).astype(BF16)
            for c in range(inputs.shape[0])
        ]
    )


def expand(shrunk, expand_table, adapter_ids):
    chats = adapter_ids.shape[0]
    parts = shrunk.reshape(chats, -1, shrunk.shape[-1])
    return [
        jnp.dot(parts[c], expand_table[adapter_ids[c]], preferred_element_type=F32)
        for c in range(chats)
    ]


def ring(n):
    right = [(i, (i + 1) % n) for i in range(n)]
    left = [(i, (i - 1) % n) for i in range(n)]

    def local(inputs, base_weight, shrink_table, expand_table, adapter_ids):
        chats, span, width = inputs.shape
        here = lax.axis_index("tensor")
        own = inputs.reshape(chats * span, width)

        def product(block, owner, first=0):
            rows = lax.dynamic_slice_in_dim(
                base_weight, lax.rem(owner + 2 * n, n) * width + first, block.shape[1], axis=0
            )
            return jnp.dot(block, rows, preferred_element_type=F32)

        shrunk = lax.psum(shrink(inputs, shrink_table, adapter_ids), "tensor")
        total = product(own, here)
        from_left = from_right = own
        for step in range(1, (n - 1) // 2 + 1):
            from_left = lax.ppermute(from_left, "tensor", right)
            from_right = lax.ppermute(from_right, "tensor", left)
            total = total + product(from_left, here - step)
            total = total + product(from_right, here + step)
        if n > 1 and n % 2 == 0:
            half = width // 2
            one = lax.ppermute(from_left[:, :half], "tensor", right)
            two = lax.ppermute(from_right[:, half:], "tensor", left)
            total = total + product(one, here - n // 2)
            total = total + product(two, here - n // 2, half)
        total = total + jnp.concatenate(expand(shrunk, expand_table, adapter_ids))
        return total.astype(BF16).reshape(chats, span, -1)

    return local


INWARD = [(0, 1), (3, 2)]
OUTWARD = [(1, 0), (2, 3)]
ACROSS = [(1, 2), (2, 1)]
SWAP = INWARD + OUTWARD


def send(block, pairs):
    return lax.ppermute(block, "tensor", pairs)


def after(block, *earlier):
    return lax.optimization_barrier((block,) + earlier)[0]


def line(inputs, base_weight, shrink_table, expand_table, adapter_ids):
    chats, span, width = inputs.shape
    rows = chats * span
    here = lax.axis_index("tensor")
    is_end = (here == 0) | (here == 3)
    far_mid = jnp.where(here < 2, 2, 1)
    far_end = jnp.where(here < 2, 3, 0)
    own = inputs.reshape(rows, width)
    half, last = width // 2, width // 8

    def product(block, owner, first=0):
        part = lax.dynamic_slice_in_dim(base_weight, owner * width + first, block.shape[1], axis=0)
        return jnp.dot(block, part, preferred_element_type=F32)

    mate = send(own, SWAP)
    mid = [send(own[:, :half], ACROSS)]
    partial = shrink(inputs, shrink_table, adapter_ids)
    mid.append(send(after(own, partial)[:, half:], ACROSS))
    mate_partial = send(partial, INWARD)
    total = product(own, here)

    mid_out = [send(after(mid[0], total), OUTWARD)]
    mate, mate_partial = lax.optimization_barrier((mate, mate_partial, mid[1], total))[:2]
    both = send(jnp.stack([partial, mate_partial]), ACROSS)
    end = [send(mate[:, :half], ACROSS)]
    end.append(send(after(mate, end[0])[:, half:], ACROSS))
    mid_out.append(send(mid[1], OUTWARD))
    total = total + product(mate, here ^ 1)

    end[0], both = lax.optimization_barrier((end[0], both, total))[:2]
    end_out = [send(end[0], OUTWARD)]
    shrunk = (
        partial.astype(F32) + mate_partial.astype(F32) + both[0].astype(F32) + both[1].astype(F32)
    ).astype(BF16)
    shrunk = jnp.where(is_end, send(shrunk, OUTWARD), shrunk)
    total = total + product(jnp.where(is_end, mid_out[0], mid[0]), far_mid)

    late = after(end[1], total)
    shrunk = after(shrunk, late)
    end_out += [send(late[:, : half - last], OUTWARD), send(late[:, half - last :], OUTWARD)]
    total = total + product(jnp.where(is_end, mid_out[1], mid[1]), far_mid, half)
    total = total + jnp.concatenate(expand(shrunk, expand_table, adapter_ids))
    total = total + product(jnp.where(is_end, end_out[0], end[0]), far_end)
    block = jnp.where(is_end, after(end_out[1], total), late[:, : half - last])
    total = total + product(block, far_end, half)
    block = jnp.where(is_end, after(end_out[2], total), late[:, half - last :])
    total = total + product(block, far_end, width - last)
    return total.astype(BF16).reshape(chats, span, -1)


def solution(mesh):
    n = mesh.shape["tensor"]
    return jax.shard_map(
        line if n == 4 else ring(n),
        mesh=mesh,
        in_specs=(
            P(("groups", "dp"), "seq", "tensor"),
            P(None, "tensor"),
            P("groups", "tensor", None),
            P("groups", None, "tensor"),
            P(("groups", "dp")),
        ),
        out_specs=P(("groups", "dp"), "seq", "tensor"),
        check_vma=False,
    )
```

```python
import jax
import jax.numpy as jnp
from jax import lax
from jax.sharding import PartitionSpec as P

F32, BF16 = jnp.float32, jnp.bfloat16


def shrink(inputs, shrink_table, adapter_ids):
    return jnp.concatenate(
        [
            jnp.dot(inputs[c], shrink_table[adapter_ids[c]], preferred_element_type=F32).astype(BF16)
            for c in range(inputs.shape[0])
        ]
    )


def expand(shrunk, expand_table, adapter_ids):
    chats = adapter_ids.shape[0]
    parts = shrunk.reshape(chats, -1, shrunk.shape[-1])
    return [
        jnp.dot(parts[c], expand_table[adapter_ids[c]], preferred_element_type=F32)
        for c in range(chats)
    ]


def ring(n):
    right = [(i, (i + 1) % n) for i in range(n)]
    left = [(i, (i - 1) % n) for i in range(n)]

    def local(inputs, base_weight, shrink_table, expand_table, adapter_ids):
        chats, span, width = inputs.shape
        here = lax.axis_index("tensor")
        own = inputs.reshape(chats * span, width)

        def product(block, owner, first=0):
            rows = lax.dynamic_slice_in_dim(
                base_weight, lax.rem(owner + 2 * n, n) * width + first, block.shape[1], axis=0
            )
            return jnp.dot(block, rows, preferred_element_type=F32)

        shrunk = lax.psum(shrink(inputs, shrink_table, adapter_ids), "tensor")
        total = product(own, here)
        from_left = from_right = own
        for step in range(1, (n - 1) // 2 + 1):
            from_left = lax.ppermute(from_left, "tensor", right)
            from_right = lax.ppermute(from_right, "tensor", left)
            total = total + product(from_left, here - step)
            total = total + product(from_right, here + step)
        if n > 1 and n % 2 == 0:
            half = width // 2
            one = lax.ppermute(from_left[:, :half], "tensor", right)
            two = lax.ppermute(from_right[:, half:], "tensor", left)
            total = total + product(one, here - n // 2)
            total = total + product(two, here - n // 2, half)
        total = total + jnp.concatenate(expand(shrunk, expand_table, adapter_ids))
        return total.astype(BF16).reshape(chats, span, -1)

    return local


INWARD = [(0, 1), (3, 2)]
OUTWARD = [(1, 0), (2, 3)]
ACROSS = [(1, 2), (2, 1)]
SWAP = INWARD + OUTWARD


def send(block, pairs):
    return lax.ppermute(block, "tensor", pairs)


def after(block, *earlier):
    return lax.optimization_barrier((block,) + earlier)[0]


def line(inputs, base_weight, shrink_table, expand_table, adapter_ids):
    chats, span, width = inputs.shape
    rows = chats * span
    here = lax.axis_index("tensor")
    is_end = (here == 0) | (here == 3)
    far_mid = jnp.where(here < 2, 2, 1)
    far_end = jnp.where(here < 2, 3, 0)
    own = inputs.reshape(rows, width)
    half, last = width // 2, width // 8

    def product(block, owner, first=0):
        part = lax.dynamic_slice_in_dim(base_weight, owner * width + first, block.shape[1], axis=0)
        return jnp.dot(block, part, preferred_element_type=F32)

    mate = send(own, SWAP)
    mid = [send(own[:, :half], ACROSS)]
    partial = shrink(inputs, shrink_table, adapter_ids)
    mid.append(send(after(own, partial)[:, half:], ACROSS))
    mate_partial = send(partial, INWARD)
    total = product(own, here)

    mid_out = [send(after(mid[0], total), OUTWARD)]
    mate, mate_partial = lax.optimization_barrier((mate, mate_partial, mid[0], total))[:2]
    both = send(jnp.stack([partial, mate_partial]), ACROSS)
    end = [send(mate[:, :half], ACROSS)]
    end.append(send(after(mate, end[0])[:, half:], ACROSS))
    mid_out.append(send(mid[1], OUTWARD))
    total = total + product(mate, here ^ 1)

    end[0], both = lax.optimization_barrier((end[0], both, total))[:2]
    end_out = [send(end[0], OUTWARD)]
    shrunk = (
        partial.astype(F32) + mate_partial.astype(F32) + both[0].astype(F32) + both[1].astype(F32)
    ).astype(BF16)
    shrunk = jnp.where(is_end, send(shrunk, OUTWARD), shrunk)
    total = total + product(jnp.where(is_end, mid_out[0], mid[0]), far_mid)

    late = after(end[1], total)
    shrunk = after(shrunk, late)
    end_out += [send(late[:, : half - last], OUTWARD), send(late[:, half - last :], OUTWARD)]
    total = total + product(jnp.where(is_end, mid_out[1], mid[1]), far_mid, half)
    total = total + jnp.concatenate(expand(shrunk, expand_table, adapter_ids))
    total = total + product(jnp.where(is_end, end_out[0], end[0]), far_end)
    block = jnp.where(is_end, after(end_out[1], total), late[:, : half - last])
    total = total + product(block, far_end, half)
    block = jnp.where(is_end, after(end_out[2], total), late[:, half - last :])
    total = total + product(block, far_end, width - last)
    return total.astype(BF16).reshape(chats, span, -1)


def solution(mesh):
    n = mesh.shape["tensor"]
    return jax.shard_map(
        line if n == 4 else ring(n),
        mesh=mesh,
        in_specs=(
            P(("groups", "dp"), "seq", "tensor"),
            P(None, "tensor"),
            P("groups", "tensor", None),
            P("groups", None, "tensor"),
            P(("groups", "dp")),
        ),
        out_specs=P(("groups", "dp"), "seq", "tensor"),
        check_vma=False,
    )
```

```python
import jax
import jax.numpy as jnp
from jax import lax
from jax.sharding import PartitionSpec as P

F32, BF16 = jnp.float32, jnp.bfloat16


def shrink(inputs, shrink_table, adapter_ids):
    return jnp.concatenate(
        [
            jnp.dot(inputs[c], shrink_table[adapter_ids[c]], preferred_element_type=F32).astype(BF16)
            for c in range(inputs.shape[0])
        ]
    )


def expand(shrunk, expand_table, adapter_ids):
    chats = adapter_ids.shape[0]
    parts = shrunk.reshape(chats, -1, shrunk.shape[-1])
    return [
        jnp.dot(parts[c], expand_table[adapter_ids[c]], preferred_element_type=F32)
        for c in range(chats)
    ]


def ring(n):
    right = [(i, (i + 1) % n) for i in range(n)]
    left = [(i, (i - 1) % n) for i in range(n)]

    def local(inputs, base_weight, shrink_table, expand_table, adapter_ids):
        chats, span, width = inputs.shape
        here = lax.axis_index("tensor")
        own = inputs.reshape(chats * span, width)

        def product(block, owner, first=0):
            rows = lax.dynamic_slice_in_dim(
                base_weight, lax.rem(owner + 2 * n, n) * width + first, block.shape[1], axis=0
            )
            return jnp.dot(block, rows, preferred_element_type=F32)

        shrunk = lax.psum(shrink(inputs, shrink_table, adapter_ids), "tensor")
        total = product(own, here)
        from_left = from_right = own
        for step in range(1, (n - 1) // 2 + 1):
            from_left = lax.ppermute(from_left, "tensor", right)
            from_right = lax.ppermute(from_right, "tensor", left)
            total = total + product(from_left, here - step)
            total = total + product(from_right, here + step)
        if n > 1 and n % 2 == 0:
            half = width // 2
            one = lax.ppermute(from_left[:, :half], "tensor", right)
            two = lax.ppermute(from_right[:, half:], "tensor", left)
            total = total + product(one, here - n // 2)
            total = total + product(two, here - n // 2, half)
        total = total + jnp.concatenate(expand(shrunk, expand_table, adapter_ids))
        return total.astype(BF16).reshape(chats, span, -1)

    return local


INWARD = [(0, 1), (3, 2)]
OUTWARD = [(1, 0), (2, 3)]
ACROSS = [(1, 2), (2, 1)]
SWAP = INWARD + OUTWARD


def send(block, pairs):
    return lax.ppermute(block, "tensor", pairs)


def after(block, *earlier):
    return lax.optimization_barrier((block,) + earlier)[0]


def line(inputs, base_weight, shrink_table, expand_table, adapter_ids):
    chats, span, width = inputs.shape
    rows = chats * span
    here = lax.axis_index("tensor")
    is_end = (here == 0) | (here == 3)
    far_mid = jnp.where(here < 2, 2, 1)
    far_end = jnp.where(here < 2, 3, 0)
    own = inputs.reshape(rows, width)
    half, last = width // 2, width // 8

    def product(block, owner, first=0):
        part = lax.dynamic_slice_in_dim(base_weight, owner * width + first, block.shape[1], axis=0)
        return jnp.dot(block, part, preferred_element_type=F32)

    mate = send(own, SWAP)
    mid = [send(own[:, :half], ACROSS)]
    partial = shrink(inputs, shrink_table, adapter_ids)
    mid.append(send(after(own, partial)[:, half:], ACROSS))
    mate_partial = send(partial, INWARD)
    total = product(own, here)

    mid_out = [send(after(mid[0], total), OUTWARD)]
    mate, mate_partial = lax.optimization_barrier((mate, mate_partial, mid[0], total))[:2]
    first, second = mate[:, :half], mate[:, half:]
    both = send(jnp.stack([partial, mate_partial]), ACROSS)
    end = [send(first, ACROSS)]
    mid_out.append(send(after(mid[1], first), OUTWARD))
    total = total + product(mate, here ^ 1)
    end.append(send(after(second, total), ACROSS))

    end[0], both = lax.optimization_barrier((end[0], both, total))[:2]
    end_out = [send(end[0], OUTWARD)]
    shrunk = (
        partial.astype(F32) + mate_partial.astype(F32) + both[0].astype(F32) + both[1].astype(F32)
    ).astype(BF16)
    shrunk = jnp.where(is_end, send(shrunk, OUTWARD), shrunk)
    total = total + product(jnp.where(is_end, mid_out[0], mid[0]), far_mid)

    late = after(end[1], total)
    shrunk = after(shrunk, late)
    end_out += [send(late[:, : half - last], OUTWARD), send(late[:, half - last :], OUTWARD)]
    total = total + product(jnp.where(is_end, mid_out[1], mid[1]), far_mid, half)
    total = total + jnp.concatenate(expand(shrunk, expand_table, adapter_ids))
    total = total + product(jnp.where(is_end, end_out[0], end[0]), far_end)
    block = jnp.where(is_end, after(end_out[1], total), late[:, : half - last])
    total = total + product(block, far_end, half)
    block = jnp.where(is_end, after(end_out[2], total), late[:, half - last :])
    total = total + product(block, far_end, width - last)
    return total.astype(BF16).reshape(chats, span, -1)


def solution(mesh):
    n = mesh.shape["tensor"]
    return jax.shard_map(
        line if n == 4 else ring(n),
        mesh=mesh,
        in_specs=(
            P(("groups", "dp"), "seq", "tensor"),
            P(None, "tensor"),
            P("groups", "tensor", None),
            P("groups", None, "tensor"),
            P(("groups", "dp")),
        ),
        out_specs=P(("groups", "dp"), "seq", "tensor"),
        check_vma=False,
    )
```

```python
import jax
import jax.numpy as jnp
from jax import lax
from jax.sharding import PartitionSpec as P

F32, BF16 = jnp.float32, jnp.bfloat16


def shrink(inputs, shrink_table, adapter_ids):
    return jnp.concatenate(
        [
            jnp.dot(inputs[c], shrink_table[adapter_ids[c]], preferred_element_type=F32).astype(BF16)
            for c in range(inputs.shape[0])
        ]
    )


def expand(shrunk, expand_table, adapter_ids):
    chats = adapter_ids.shape[0]
    parts = shrunk.reshape(chats, -1, shrunk.shape[-1])
    return [
        jnp.dot(parts[c], expand_table[adapter_ids[c]], preferred_element_type=F32)
        for c in range(chats)
    ]


def ring(n):
    right = [(i, (i + 1) % n) for i in range(n)]
    left = [(i, (i - 1) % n) for i in range(n)]

    def local(inputs, base_weight, shrink_table, expand_table, adapter_ids):
        chats, span, width = inputs.shape
        here = lax.axis_index("tensor")
        own = inputs.reshape(chats * span, width)

        def product(block, owner, first=0):
            rows = lax.dynamic_slice_in_dim(
                base_weight, lax.rem(owner + 2 * n, n) * width + first, block.shape[1], axis=0
            )
            return jnp.dot(block, rows, preferred_element_type=F32)

        shrunk = lax.psum(shrink(inputs, shrink_table, adapter_ids), "tensor")
        total = product(own, here)
        from_left = from_right = own
        for step in range(1, (n - 1) // 2 + 1):
            from_left = lax.ppermute(from_left, "tensor", right)
            from_right = lax.ppermute(from_right, "tensor", left)
            total = total + product(from_left, here - step)
            total = total + product(from_right, here + step)
        if n > 1 and n % 2 == 0:
            half = width // 2
            one = lax.ppermute(from_left[:, :half], "tensor", right)
            two = lax.ppermute(from_right[:, half:], "tensor", left)
            total = total + product(one, here - n // 2)
            total = total + product(two, here - n // 2, half)
        total = total + jnp.concatenate(expand(shrunk, expand_table, adapter_ids))
        return total.astype(BF16).reshape(chats, span, -1)

    return local


INWARD = [(0, 1), (3, 2)]
OUTWARD = [(1, 0), (2, 3)]
ACROSS = [(1, 2), (2, 1)]


def send(block, pairs):
    return lax.ppermute(block, "tensor", pairs)


def after(block, *earlier):
    return lax.optimization_barrier((block,) + earlier)[0]


def line(inputs, base_weight, shrink_table, expand_table, adapter_ids):
    chats, span, width = inputs.shape
    rows = chats * span
    here = lax.axis_index("tensor")
    is_end = (here == 0) | (here == 3)
    far_mid = jnp.where(here < 2, 2, 1)
    far_end = jnp.where(here < 2, 3, 0)
    own = inputs.reshape(rows, width)
    half, last = width // 2, width // 8

    def product(block, owner, first=0):
        part = lax.dynamic_slice_in_dim(base_weight, owner * width + first, block.shape[1], axis=0)
        return jnp.dot(block, part, preferred_element_type=F32)

    mate_out = send(own, OUTWARD)
    piece = own[:, :half]
    mate_in = [send(piece, INWARD)]
    mid = [send(piece, ACROSS)]
    partial = shrink(inputs, shrink_table, adapter_ids)
    piece = after(own, partial)[:, half:]
    mate_in.append(send(piece, INWARD))
    mid.append(send(piece, ACROSS))
    mate_partial = send(partial, INWARD)
    total = product(own, here)

    mid_out = [send(after(mid[0], total), OUTWARD)]
    end = [send(after(mate_in[0], total), ACROSS)]
    mate_in[1], mate_partial = lax.optimization_barrier((mate_in[1], mate_partial, mid[0]))[:2]
    both = send(jnp.stack([partial, mate_partial]), ACROSS)
    end.append(send(mate_in[1], ACROSS))
    mid_out.append(send(mid[1], OUTWARD))

    end_out = [send(end[0], OUTWARD)]
    mate_out, both = lax.optimization_barrier((mate_out, both, end[0], mid[1]))[:2]
    total = total + product(jnp.where(is_end, mate_out[:, :half], mate_in[0]), here ^ 1)
    total = total + product(jnp.where(is_end, mate_out[:, half:], mate_in[1]), here ^ 1, half)
    shrunk = (
        partial.astype(F32) + mate_partial.astype(F32) + both[0].astype(F32) + both[1].astype(F32)
    ).astype(BF16)
    shrunk = jnp.where(is_end, send(shrunk, OUTWARD), shrunk)
    total = total + product(jnp.where(is_end, mid_out[0], mid[0]), far_mid)

    late = after(end[1], total)
    shrunk, mid_out[1] = lax.optimization_barrier((shrunk, mid_out[1], late))[:2]
    end_out += [send(late[:, : half - last], OUTWARD), send(late[:, half - last :], OUTWARD)]
    total = total + product(jnp.where(is_end, mid_out[1], mid[1]), far_mid, half)
    total = total + jnp.concatenate(expand(shrunk, expand_table, adapter_ids))
    total = total + product(jnp.where(is_end, after(end_out[0], total), end[0]), far_end)
    block = jnp.where(is_end, after(end_out[1], total), late[:, : half - last])
    total = total + product(block, far_end, half)
    block = jnp.where(is_end, after(end_out[2], total), late[:, half - last :])
    total = total + product(block, far_end, width - last)
    return total.astype(BF16).reshape(chats, span, -1)


def solution(mesh):
    n = mesh.shape["tensor"]
    return jax.shard_map(
        line if n == 4 else ring(n),
        mesh=mesh,
        in_specs=(
            P(("groups", "dp"), "seq", "tensor"),
            P(None, "tensor"),
            P("groups", "tensor", None),
            P("groups", None, "tensor"),
            P(("groups", "dp")),
        ),
        out_specs=P(("groups", "dp"), "seq", "tensor"),
        check_vma=False,
    )
```

```python
import jax
import jax.numpy as jnp
from jax import lax
from jax.sharding import PartitionSpec as P

F32, BF16 = jnp.float32, jnp.bfloat16


def shrink(inputs, shrink_table, adapter_ids):
    return jnp.concatenate(
        [
            jnp.dot(inputs[c], shrink_table[adapter_ids[c]], preferred_element_type=F32).astype(BF16)
            for c in range(inputs.shape[0])
        ]
    )


def expand(shrunk, expand_table, adapter_ids):
    chats = adapter_ids.shape[0]
    parts = shrunk.reshape(chats, -1, shrunk.shape[-1])
    return [
        jnp.dot(parts[c], expand_table[adapter_ids[c]], preferred_element_type=F32)
        for c in range(chats)
    ]


def ring(n):
    right = [(i, (i + 1) % n) for i in range(n)]
    left = [(i, (i - 1) % n) for i in range(n)]

    def local(inputs, base_weight, shrink_table, expand_table, adapter_ids):
        chats, span, width = inputs.shape
        here = lax.axis_index("tensor")
        own = inputs.reshape(chats * span, width)

        def product(block, owner, first=0):
            rows = lax.dynamic_slice_in_dim(
                base_weight, lax.rem(owner + 2 * n, n) * width + first, block.shape[1], axis=0
            )
            return jnp.dot(block, rows, preferred_element_type=F32)

        shrunk = lax.psum(shrink(inputs, shrink_table, adapter_ids), "tensor")
        total = product(own, here)
        from_left = from_right = own
        for step in range(1, (n - 1) // 2 + 1):
            from_left = lax.ppermute(from_left, "tensor", right)
            from_right = lax.ppermute(from_right, "tensor", left)
            total = total + product(from_left, here - step)
            total = total + product(from_right, here + step)
        if n > 1 and n % 2 == 0:
            half = width // 2
            one = lax.ppermute(from_left[:, :half], "tensor", right)
            two = lax.ppermute(from_right[:, half:], "tensor", left)
            total = total + product(one, here - n // 2)
            total = total + product(two, here - n // 2, half)
        total = total + jnp.concatenate(expand(shrunk, expand_table, adapter_ids))
        return total.astype(BF16).reshape(chats, span, -1)

    return local


INWARD = [(0, 1), (3, 2)]
OUTWARD = [(1, 0), (2, 3)]
ACROSS = [(1, 2), (2, 1)]
SWAP = INWARD + OUTWARD


def send(block, pairs):
    return lax.ppermute(block, "tensor", pairs)


def after(block, *earlier):
    return lax.optimization_barrier((block,) + earlier)[0]


def line(inputs, base_weight, shrink_table, expand_table, adapter_ids):
    chats, span, width = inputs.shape
    rows = chats * span
    here = lax.axis_index("tensor")
    is_end = (here == 0) | (here == 3)
    far_mid = jnp.where(here < 2, 2, 1)
    far_end = jnp.where(here < 2, 3, 0)
    own = inputs.reshape(rows, width)
    half, last = width // 2, width // 8

    def product(block, owner, first=0):
        part = lax.dynamic_slice_in_dim(base_weight, owner * width + first, block.shape[1], axis=0)
        return jnp.dot(block, part, preferred_element_type=F32)

    mate = send(own, SWAP)
    mid = [send(own[:, :half], ACROSS)]
    partial = shrink(inputs, shrink_table, adapter_ids)
    mid.append(send(after(own, partial)[:, half:], ACROSS))
    mate_partial = send(partial, INWARD)
    total = product(own, here)

    mid_out = [send(after(mid[0], total), OUTWARD)]
    mate, mate_partial = lax.optimization_barrier((mate, mate_partial, mid[1], total))[:2]
    both = send(jnp.stack([partial, mate_partial]), ACROSS)
    end = [send(mate[:, :half], ACROSS)]
    end.append(send(after(mate, mid_out[0])[:, half:], ACROSS))
    mid_out.append(send(mid[1], OUTWARD))
    total = total + product(mate, here ^ 1)

    end[0], both = lax.optimization_barrier((end[0], both, total))[:2]
    end_out = [send(end[0], OUTWARD)]
    shrunk = (
        partial.astype(F32) + mate_partial.astype(F32) + both[0].astype(F32) + both[1].astype(F32)
    ).astype(BF16)
    shrunk = jnp.where(is_end, send(shrunk, OUTWARD), shrunk)
    total = total + product(jnp.where(is_end, mid_out[0], mid[0]), far_mid)

    late = after(end[1], total)
    shrunk = after(shrunk, late)
    end_out += [send(late[:, : half - last], OUTWARD), send(late[:, half - last :], OUTWARD)]
    total = total + product(jnp.where(is_end, mid_out[1], mid[1]), far_mid, half)
    total = total + jnp.concatenate(expand(shrunk, expand_table, adapter_ids))
    total = total + product(jnp.where(is_end, end_out[0], end[0]), far_end)
    block = jnp.where(is_end, after(end_out[1], total), late[:, : half - last])
    total = total + product(block, far_end, half)
    block = jnp.where(is_end, after(end_out[2], total), late[:, half - last :])
    total = total + product(block, far_end, width - last)
    return total.astype(BF16).reshape(chats, span, -1)


def solution(mesh):
    n = mesh.shape["tensor"]
    return jax.shard_map(
        line if n == 4 else ring(n),
        mesh=mesh,
        in_specs=(
            P(("groups", "dp"), "seq", "tensor"),
            P(None, "tensor"),
            P("groups", "tensor", None),
            P("groups", None, "tensor"),
            P(("groups", "dp")),
        ),
        out_specs=P(("groups", "dp"), "seq", "tensor"),
        check_vma=False,
    )
```

```python
import jax
import jax.numpy as jnp
from jax import lax
from jax.sharding import PartitionSpec as P

F32, BF16 = jnp.float32, jnp.bfloat16


def shrink(inputs, shrink_table, adapter_ids):
    return jnp.concatenate(
        [
            jnp.dot(inputs[c], shrink_table[adapter_ids[c]], preferred_element_type=F32).astype(BF16)
            for c in range(inputs.shape[0])
        ]
    )


def expand(shrunk, expand_table, adapter_ids):
    chats = adapter_ids.shape[0]
    parts = shrunk.reshape(chats, -1, shrunk.shape[-1])
    return [
        jnp.dot(parts[c], expand_table[adapter_ids[c]], preferred_element_type=F32)
        for c in range(chats)
    ]


def ring(n):
    right = [(i, (i + 1) % n) for i in range(n)]
    left = [(i, (i - 1) % n) for i in range(n)]

    def local(inputs, base_weight, shrink_table, expand_table, adapter_ids):
        chats, span, width = inputs.shape
        here = lax.axis_index("tensor")
        own = inputs.reshape(chats * span, width)

        def product(block, owner, first=0):
            rows = lax.dynamic_slice_in_dim(
                base_weight, lax.rem(owner + 2 * n, n) * width + first, block.shape[1], axis=0
            )
            return jnp.dot(block, rows, preferred_element_type=F32)

        shrunk = lax.psum(shrink(inputs, shrink_table, adapter_ids), "tensor")
        total = product(own, here)
        from_left = from_right = own
        for step in range(1, (n - 1) // 2 + 1):
            from_left = lax.ppermute(from_left, "tensor", right)
            from_right = lax.ppermute(from_right, "tensor", left)
            total = total + product(from_left, here - step)
            total = total + product(from_right, here + step)
        if n > 1 and n % 2 == 0:
            half = width // 2
            one = lax.ppermute(from_left[:, :half], "tensor", right)
            two = lax.ppermute(from_right[:, half:], "tensor", left)
            total = total + product(one, here - n // 2)
            total = total + product(two, here - n // 2, half)
        total = total + jnp.concatenate(expand(shrunk, expand_table, adapter_ids))
        return total.astype(BF16).reshape(chats, span, -1)

    return local


INWARD = [(0, 1), (3, 2)]
OUTWARD = [(1, 0), (2, 3)]
ACROSS = [(1, 2), (2, 1)]
SWAP = INWARD + OUTWARD


def send(block, pairs):
    return lax.ppermute(block, "tensor", pairs)


def after(block, *earlier):
    return lax.optimization_barrier((block,) + earlier)[0]


def line(inputs, base_weight, shrink_table, expand_table, adapter_ids):
    chats, span, width = inputs.shape
    rows = chats * span
    here = lax.axis_index("tensor")
    is_end = (here == 0) | (here == 3)
    far_mid = jnp.where(here < 2, 2, 1)
    far_end = jnp.where(here < 2, 3, 0)
    own = inputs.reshape(rows, width)
    half, last = width // 2, width // 8

    def product(block, owner, first=0):
        part = lax.dynamic_slice_in_dim(base_weight, owner * width + first, block.shape[1], axis=0)
        return jnp.dot(block, part, preferred_element_type=F32)

    mate = send(own, SWAP)
    mid = [send(own[:, :half], ACROSS)]
    partial = shrink(inputs, shrink_table, adapter_ids)
    mid.append(send(after(own, partial)[:, half:], ACROSS))
    mate_partial = send(partial, INWARD)
    total = product(own, here)

    mid_out = [send(after(mid[0], total), OUTWARD)]
    mate, mate_partial = lax.optimization_barrier((mate, mate_partial, mid[0], total))[:2]
    both = send(jnp.stack([partial, mate_partial]), ACROSS)
    first = mate[:, :half]
    end = [send(first, ACROSS)]
    end.append(send(after(mate, end[0])[:, half:], ACROSS))
    mid_out.append(send(after(mid[1], first), OUTWARD))
    total = total + product(mate, here ^ 1)

    end[0], both = lax.optimization_barrier((end[0], both, total))[:2]
    end_out = [send(end[0], OUTWARD)]
    shrunk = (
        partial.astype(F32) + mate_partial.astype(F32) + both[0].astype(F32) + both[1].astype(F32)
    ).astype(BF16)
    shrunk = jnp.where(is_end, send(shrunk, OUTWARD), shrunk)
    total = total + product(jnp.where(is_end, mid_out[0], mid[0]), far_mid)

    late = after(end[1], total)
    shrunk = after(shrunk, late)
    end_out += [send(late[:, : half - last], OUTWARD), send(late[:, half - last :], OUTWARD)]
    total = total + product(jnp.where(is_end, mid_out[1], mid[1]), far_mid, half)
    total = total + jnp.concatenate(expand(shrunk, expand_table, adapter_ids))
    total = total + product(jnp.where(is_end, end_out[0], end[0]), far_end)
    block = jnp.where(is_end, after(end_out[1], total), late[:, : half - last])
    total = total + product(block, far_end, half)
    block = jnp.where(is_end, after(end_out[2], total), late[:, half - last :])
    total = total + product(block, far_end, width - last)
    return total.astype(BF16).reshape(chats, span, -1)


def solution(mesh):
    n = mesh.shape["tensor"]
    return jax.shard_map(
        line if n == 4 else ring(n),
        mesh=mesh,
        in_specs=(
            P(("groups", "dp"), "seq", "tensor"),
            P(None, "tensor"),
            P("groups", "tensor", None),
            P("groups", None, "tensor"),
            P(("groups", "dp")),
        ),
        out_specs=P(("groups", "dp"), "seq", "tensor"),
        check_vma=False,
    )
```

```python
import jax
import jax.numpy as jnp
from jax import lax
from jax.sharding import PartitionSpec as P

F32, BF16 = jnp.float32, jnp.bfloat16


def shrink(inputs, shrink_table, adapter_ids):
    return jnp.concatenate(
        [
            jnp.dot(inputs[c], shrink_table[adapter_ids[c]], preferred_element_type=F32).astype(BF16)
            for c in range(inputs.shape[0])
        ]
    )


def expand(shrunk, expand_table, adapter_ids):
    chats = adapter_ids.shape[0]
    parts = shrunk.reshape(chats, -1, shrunk.shape[-1])
    return [
        jnp.dot(parts[c], expand_table[adapter_ids[c]], preferred_element_type=F32)
        for c in range(chats)
    ]


def ring(n):
    right = [(i, (i + 1) % n) for i in range(n)]
    left = [(i, (i - 1) % n) for i in range(n)]

    def local(inputs, base_weight, shrink_table, expand_table, adapter_ids):
        chats, span, width = inputs.shape
        here = lax.axis_index("tensor")
        own = inputs.reshape(chats * span, width)

        def product(block, owner, first=0):
            rows = lax.dynamic_slice_in_dim(
                base_weight, lax.rem(owner + 2 * n, n) * width + first, block.shape[1], axis=0
            )
            return jnp.dot(block, rows, preferred_element_type=F32)

        shrunk = lax.psum(shrink(inputs, shrink_table, adapter_ids), "tensor")
        total = product(own, here)
        from_left = from_right = own
        for step in range(1, (n - 1) // 2 + 1):
            from_left = lax.ppermute(from_left, "tensor", right)
            from_right = lax.ppermute(from_right, "tensor", left)
            total = total + product(from_left, here - step)
            total = total + product(from_right, here + step)
        if n > 1 and n % 2 == 0:
            half = width // 2
            one = lax.ppermute(from_left[:, :half], "tensor", right)
            two = lax.ppermute(from_right[:, half:], "tensor", left)
            total = total + product(one, here - n // 2)
            total = total + product(two, here - n // 2, half)
        total = total + jnp.concatenate(expand(shrunk, expand_table, adapter_ids))
        return total.astype(BF16).reshape(chats, span, -1)

    return local


INWARD = [(0, 1), (3, 2)]
OUTWARD = [(1, 0), (2, 3)]
ACROSS = [(1, 2), (2, 1)]
SWAP = INWARD + OUTWARD


def send(block, pairs):
    return lax.ppermute(block, "tensor", pairs)


def after(block, *earlier):
    return lax.optimization_barrier((block,) + earlier)[0]


def line(inputs, base_weight, shrink_table, expand_table, adapter_ids):
    chats, span, width = inputs.shape
    rows = chats * span
    here = lax.axis_index("tensor")
    is_end = (here == 0) | (here == 3)
    far_mid = jnp.where(here < 2, 2, 1)
    far_end = jnp.where(here < 2, 3, 0)
    own = inputs.reshape(rows, width)
    half, quarter = width // 2, width // 4

    def product(block, owner, first=0):
        part = lax.dynamic_slice_in_dim(base_weight, owner * width + first, block.shape[1], axis=0)
        return jnp.dot(block, part, preferred_element_type=F32)

    mate = send(own, SWAP)
    mid = [send(own[:, :half], ACROSS)]
    partial = shrink(inputs, shrink_table, adapter_ids)
    mid.append(send(after(own, partial)[:, half:], ACROSS))
    mate_partial = send(partial, INWARD)
    total = product(own, here)

    mid_out = [send(after(mid[0], total), OUTWARD)]
    mate, mate_partial = lax.optimization_barrier((mate, mate_partial, mid[0], total))[:2]
    both = send(jnp.stack([partial, mate_partial]), ACROSS)
    first = mate[:, :half]
    end = [send(first, ACROSS)]
    end.append(send(after(mate, end[0])[:, half:], ACROSS))
    mid_out.append(send(after(mid[1], first), OUTWARD))
    total = total + product(mate, here ^ 1)

    end[0], both = lax.optimization_barrier((end[0], both, total))[:2]
    end_out = [send(end[0], OUTWARD)]
    shrunk = (
        partial.astype(F32) + mate_partial.astype(F32) + both[0].astype(F32) + both[1].astype(F32)
    ).astype(BF16)
    total = total + product(jnp.where(is_end, mid_out[0], mid[0]), far_mid)

    late = after(end[1], total)
    rider = shrunk.reshape(-1, quarter)
    end_out += [
        send(jnp.concatenate([late[:, :quarter], rider]), OUTWARD),
        send(late[:, quarter:], OUTWARD),
    ]
    total = total + product(jnp.where(is_end, mid_out[1], mid[1]), far_mid, half)
    total = total + product(jnp.where(is_end, after(end_out[0], total), end[0]), far_end)
    ridden = after(end_out[1], total)
    shrunk = jnp.where(is_end, ridden[rows:].reshape(shrunk.shape), shrunk)
    total = total + jnp.concatenate(expand(shrunk, expand_table, adapter_ids))
    total = total + product(jnp.where(is_end, ridden[:rows], late[:, :quarter]), far_end, half)
    block = jnp.where(is_end, after(end_out[2], total), late[:, quarter:])
    total = total + product(block, far_end, half + quarter)
    return total.astype(BF16).reshape(chats, span, -1)


def solution(mesh):
    n = mesh.shape["tensor"]
    return jax.shard_map(
        line if n == 4 else ring(n),
        mesh=mesh,
        in_specs=(
            P(("groups", "dp"), "seq", "tensor"),
            P(None, "tensor"),
            P("groups", "tensor", None),
            P("groups", None, "tensor"),
            P(("groups", "dp")),
        ),
        out_specs=P(("groups", "dp"), "seq", "tensor"),
        check_vma=False,
    )
```

```python
import jax
import jax.numpy as jnp
from jax import lax
from jax.experimental import pallas as pl
from jax.experimental.pallas import tpu as pltpu
from jax.sharding import PartitionSpec as P

F32, BF16 = jnp.float32, jnp.bfloat16


def shrink(inputs, shrink_table, adapter_ids):
    return jnp.concatenate(
        [
            jnp.dot(inputs[c], shrink_table[adapter_ids[c]], preferred_element_type=F32).astype(BF16)
            for c in range(inputs.shape[0])
        ]
    )


def expand(shrunk, expand_table, adapter_ids):
    chats = adapter_ids.shape[0]
    parts = shrunk.reshape(chats, -1, shrunk.shape[-1])
    return [
        jnp.dot(parts[c], expand_table[adapter_ids[c]], preferred_element_type=F32)
        for c in range(chats)
    ]


def ring(n):
    right = [(i, (i + 1) % n) for i in range(n)]
    left = [(i, (i - 1) % n) for i in range(n)]

    def local(inputs, base_weight, shrink_table, expand_table, adapter_ids):
        chats, span, width = inputs.shape
        here = lax.axis_index("tensor")
        own = inputs.reshape(chats * span, width)

        def product(block, owner, first=0):
            rows = lax.dynamic_slice_in_dim(
                base_weight, lax.rem(owner + 2 * n, n) * width + first, block.shape[1], axis=0
            )
            return jnp.dot(block, rows, preferred_element_type=F32)

        shrunk = lax.psum(shrink(inputs, shrink_table, adapter_ids), "tensor")
        total = product(own, here)
        from_left = from_right = own
        for step in range(1, (n - 1) // 2 + 1):
            from_left = lax.ppermute(from_left, "tensor", right)
            from_right = lax.ppermute(from_right, "tensor", left)
            total = total + product(from_left, here - step)
            total = total + product(from_right, here + step)
        if n > 1 and n % 2 == 0:
            half = width // 2
            one = lax.ppermute(from_left[:, :half], "tensor", right)
            two = lax.ppermute(from_right[:, half:], "tensor", left)
            total = total + product(one, here - n // 2)
            total = total + product(two, here - n // 2, half)
        total = total + jnp.concatenate(expand(shrunk, expand_table, adapter_ids))
        return total.astype(BF16).reshape(chats, span, -1)

    return local


INWARD = [(0, 1), (3, 2)]
OUTWARD = [(1, 0), (2, 3)]
ACROSS = [(1, 2), (2, 1)]
SWAP = INWARD + OUTWARD


def send(block, pairs):
    return lax.ppermute(block, "tensor", pairs)


def after(block, *earlier):
    return lax.optimization_barrier((block,) + earlier)[0]


def resident(block, cuts):
    def kernel(source, *refs):
        outs, sems = refs[: len(cuts)], refs[len(cuts)]
        copies = [
            pltpu.make_async_copy(source.at[:, cut], out, sems.at[i])
            for i, (cut, out) in enumerate(zip(cuts, outs))
        ]
        for copy in copies:
            copy.start()
        for copy in copies:
            copy.wait()

    rows = block.shape[0]
    size = sum(cut.size for cut in cuts) * rows * block.dtype.itemsize
    return pl.pallas_call(
        kernel,
        out_shape=[pltpu.VMEM((rows, cut.size), block.dtype) for cut in cuts],
        in_specs=[pl.BlockSpec(memory_space=pl.ANY)],
        out_specs=[pl.BlockSpec(memory_space=pltpu.VMEM) for _ in cuts],
        scratch_shapes=[pltpu.SemaphoreType.DMA((len(cuts),))],
        compiler_params=pltpu.CompilerParams(vmem_limit_bytes=4 * 2**20),
        cost_estimate=pl.CostEstimate(flops=0, bytes_accessed=2 * size, transcendentals=0),
    )(block)


def line(inputs, base_weight, shrink_table, expand_table, adapter_ids):
    chats, span, width = inputs.shape
    rows = chats * span
    here = lax.axis_index("tensor")
    is_end = (here == 0) | (here == 3)
    far_mid = jnp.where(here < 2, 2, 1)
    far_end = jnp.where(here < 2, 3, 0)
    own = inputs.reshape(rows, width)
    half, last = width // 2, width // 8

    def product(block, owner, first=0):
        part = lax.dynamic_slice_in_dim(base_weight, owner * width + first, block.shape[1], axis=0)
        return jnp.dot(block, part, preferred_element_type=F32)

    whole, left, right = resident(own, [pl.ds(0, width), pl.ds(0, half), pl.ds(half, half)])
    mate = send(whole, SWAP)
    mid = [send(left, ACROSS)]
    partial = shrink(inputs, shrink_table, adapter_ids)
    mid.append(send(after(right, partial), ACROSS))
    mate_partial = send(partial, INWARD)
    total = product(own, here)

    mid_out = [send(after(mid[0], total), OUTWARD)]
    mate, mate_partial = lax.optimization_barrier((mate, mate_partial, mid[0], total))[:2]
    both = send(jnp.stack([partial, mate_partial]), ACROSS)
    first = mate[:, :half]
    end = [send(first, ACROSS)]
    end.append(send(after(mate, end[0])[:, half:], ACROSS))
    mid_out.append(send(after(mid[1], first), OUTWARD))
    total = total + product(mate, here ^ 1)

    end[0], both = lax.optimization_barrier((end[0], both, total))[:2]
    end_out = [send(end[0], OUTWARD)]
    shrunk = (
        partial.astype(F32) + mate_partial.astype(F32) + both[0].astype(F32) + both[1].astype(F32)
    ).astype(BF16)
    shrunk = jnp.where(is_end, send(shrunk, OUTWARD), shrunk)
    total = total + product(jnp.where(is_end, mid_out[0], mid[0]), far_mid)

    late = after(end[1], total)
    shrunk = after(shrunk, late)
    end_out += [send(late[:, : half - last], OUTWARD), send(late[:, half - last :], OUTWARD)]
    total = total + product(jnp.where(is_end, mid_out[1], mid[1]), far_mid, half)
    total = total + jnp.concatenate(expand(shrunk, expand_table, adapter_ids))
    total = total + product(jnp.where(is_end, end_out[0], end[0]), far_end)
    block = jnp.where(is_end, after(end_out[1], total), late[:, : half - last])
    total = total + product(block, far_end, half)
    block = jnp.where(is_end, after(end_out[2], total), late[:, half - last :])
    total = total + product(block, far_end, width - last)
    return total.astype(BF16).reshape(chats, span, -1)


def solution(mesh):
    n = mesh.shape["tensor"]
    return jax.shard_map(
        line if n == 4 else ring(n),
        mesh=mesh,
        in_specs=(
            P(("groups", "dp"), "seq", "tensor"),
            P(None, "tensor"),
            P("groups", "tensor", None),
            P("groups", None, "tensor"),
            P(("groups", "dp")),
        ),
        out_specs=P(("groups", "dp"), "seq", "tensor"),
        check_vma=False,
    )
```

```python
import jax
import jax.numpy as jnp
from jax import lax
from jax.sharding import PartitionSpec as P

F32, BF16 = jnp.float32, jnp.bfloat16


def shrink(inputs, shrink_table, adapter_ids):
    return jnp.concatenate(
        [
            jnp.dot(inputs[c], shrink_table[adapter_ids[c]], preferred_element_type=F32).astype(BF16)
            for c in range(inputs.shape[0])
        ]
    )


def expand(shrunk, expand_table, adapter_ids):
    chats = adapter_ids.shape[0]
    parts = shrunk.reshape(chats, -1, shrunk.shape[-1])
    return [
        jnp.dot(parts[c], expand_table[adapter_ids[c]], preferred_element_type=F32)
        for c in range(chats)
    ]


def ring(n):
    right = [(i, (i + 1) % n) for i in range(n)]
    left = [(i, (i - 1) % n) for i in range(n)]

    def local(inputs, base_weight, shrink_table, expand_table, adapter_ids):
        chats, span, width = inputs.shape
        here = lax.axis_index("tensor")
        own = inputs.reshape(chats * span, width)

        def product(block, owner, first=0):
            rows = lax.dynamic_slice_in_dim(
                base_weight, lax.rem(owner + 2 * n, n) * width + first, block.shape[1], axis=0
            )
            return jnp.dot(block, rows, preferred_element_type=F32)

        shrunk = lax.psum(shrink(inputs, shrink_table, adapter_ids), "tensor")
        total = product(own, here)
        from_left = from_right = own
        for step in range(1, (n - 1) // 2 + 1):
            from_left = lax.ppermute(from_left, "tensor", right)
            from_right = lax.ppermute(from_right, "tensor", left)
            total = total + product(from_left, here - step)
            total = total + product(from_right, here + step)
        if n > 1 and n % 2 == 0:
            half = width // 2
            one = lax.ppermute(from_left[:, :half], "tensor", right)
            two = lax.ppermute(from_right[:, half:], "tensor", left)
            total = total + product(one, here - n // 2)
            total = total + product(two, here - n // 2, half)
        total = total + jnp.concatenate(expand(shrunk, expand_table, adapter_ids))
        return total.astype(BF16).reshape(chats, span, -1)

    return local


INWARD = [(0, 1), (3, 2)]
OUTWARD = [(1, 0), (2, 3)]
ACROSS = [(1, 2), (2, 1)]
FAR = [(0, 2), (3, 1)]
SWAP = INWARD + OUTWARD


def send(block, pairs):
    return lax.ppermute(block, "tensor", pairs)


def after(block, *earlier):
    return lax.optimization_barrier((block,) + earlier)[0]


def line(inputs, base_weight, shrink_table, expand_table, adapter_ids):
    chats, span, width = inputs.shape
    rows = chats * span
    here = lax.axis_index("tensor")
    is_end = (here == 0) | (here == 3)
    far_mid = jnp.where(here < 2, 2, 1)
    far_end = jnp.where(here < 2, 3, 0)
    own = inputs.reshape(rows, width)
    half, last = width // 2, width // 8

    def product(block, owner, first=0):
        part = lax.dynamic_slice_in_dim(base_weight, owner * width + first, block.shape[1], axis=0)
        return jnp.dot(block, part, preferred_element_type=F32)

    mate = send(own, SWAP)
    left = own[:, :half]
    mid = [send(left, ACROSS)]
    partial = shrink(inputs, shrink_table, adapter_ids)
    left, right = after(left, partial), after(own, partial)[:, half:]
    mid.append(send(right, ACROSS))
    end = [send(left, FAR), send(right, FAR)]
    mate_partial = send(partial, INWARD)
    total = product(own, here)

    mid_out = [send(after(mid[0], total), OUTWARD)]
    mate, mate_partial = lax.optimization_barrier((mate, mate_partial, mid[1], total))[:2]
    both = send(jnp.stack([partial, mate_partial]), ACROSS)
    mid_out.append(send(mid[1], OUTWARD))
    total = total + product(mate, here ^ 1)

    end[0], both = lax.optimization_barrier((end[0], both, total))[:2]
    end_out = [send(end[0], OUTWARD)]
    shrunk = (
        partial.astype(F32) + mate_partial.astype(F32) + both[0].astype(F32) + both[1].astype(F32)
    ).astype(BF16)
    shrunk = jnp.where(is_end, send(shrunk, OUTWARD), shrunk)
    total = total + product(jnp.where(is_end, mid_out[0], mid[0]), far_mid)

    late = after(end[1], total)
    shrunk = after(shrunk, late)
    end_out += [send(late[:, : half - last], OUTWARD), send(late[:, half - last :], OUTWARD)]
    total = total + product(jnp.where(is_end, mid_out[1], mid[1]), far_mid, half)
    total = total + jnp.concatenate(expand(shrunk, expand_table, adapter_ids))
    total = total + product(jnp.where(is_end, end_out[0], end[0]), far_end)
    block = jnp.where(is_end, after(end_out[1], total), late[:, : half - last])
    total = total + product(block, far_end, half)
    block = jnp.where(is_end, after(end_out[2], total), late[:, half - last :])
    total = total + product(block, far_end, width - last)
    return total.astype(BF16).reshape(chats, span, -1)


def solution(mesh):
    n = mesh.shape["tensor"]
    return jax.shard_map(
        line if n == 4 else ring(n),
        mesh=mesh,
        in_specs=(
            P(("groups", "dp"), "seq", "tensor"),
            P(None, "tensor"),
            P("groups", "tensor", None),
            P("groups", None, "tensor"),
            P(("groups", "dp")),
        ),
        out_specs=P(("groups", "dp"), "seq", "tensor"),
        check_vma=False,
    )
```

```python
import jax
import jax.numpy as jnp
from jax import lax
from jax.sharding import PartitionSpec as P

F32, BF16 = jnp.float32, jnp.bfloat16


def shrink(inputs, shrink_table, adapter_ids):
    return jnp.concatenate(
        [
            jnp.dot(inputs[c], shrink_table[adapter_ids[c]], preferred_element_type=F32).astype(BF16)
            for c in range(inputs.shape[0])
        ]
    )


def expand(shrunk, expand_table, adapter_ids):
    chats = adapter_ids.shape[0]
    parts = shrunk.reshape(chats, -1, shrunk.shape[-1])
    return [
        jnp.dot(parts[c], expand_table[adapter_ids[c]], preferred_element_type=F32)
        for c in range(chats)
    ]


def ring(n):
    right = [(i, (i + 1) % n) for i in range(n)]
    left = [(i, (i - 1) % n) for i in range(n)]

    def local(inputs, base_weight, shrink_table, expand_table, adapter_ids):
        chats, span, width = inputs.shape
        here = lax.axis_index("tensor")
        own = inputs.reshape(chats * span, width)

        def product(block, owner, first=0):
            rows = lax.dynamic_slice_in_dim(
                base_weight, lax.rem(owner + 2 * n, n) * width + first, block.shape[1], axis=0
            )
            return jnp.dot(block, rows, preferred_element_type=F32)

        shrunk = lax.psum(shrink(inputs, shrink_table, adapter_ids), "tensor")
        total = product(own, here)
        from_left = from_right = own
        for step in range(1, (n - 1) // 2 + 1):
            from_left = lax.ppermute(from_left, "tensor", right)
            from_right = lax.ppermute(from_right, "tensor", left)
            total = total + product(from_left, here - step)
            total = total + product(from_right, here + step)
        if n > 1 and n % 2 == 0:
            half = width // 2
            one = lax.ppermute(from_left[:, :half], "tensor", right)
            two = lax.ppermute(from_right[:, half:], "tensor", left)
            total = total + product(one, here - n // 2)
            total = total + product(two, here - n // 2, half)
        total = total + jnp.concatenate(expand(shrunk, expand_table, adapter_ids))
        return total.astype(BF16).reshape(chats, span, -1)

    return local


INWARD = [(0, 1), (3, 2)]
OUTWARD = [(1, 0), (2, 3)]
ACROSS = [(1, 2), (2, 1)]
FAR = [(0, 2), (3, 1)]
SWAP = INWARD + OUTWARD


def send(block, pairs):
    return lax.ppermute(block, "tensor", pairs)


def after(block, *earlier):
    return lax.optimization_barrier((block,) + earlier)[0]


def line(inputs, base_weight, shrink_table, expand_table, adapter_ids):
    chats, span, width = inputs.shape
    rows = chats * span
    here = lax.axis_index("tensor")
    is_end = (here == 0) | (here == 3)
    far_mid = jnp.where(here < 2, 2, 1)
    far_end = jnp.where(here < 2, 3, 0)
    own = inputs.reshape(rows, width)
    half, last = width // 2, width // 8

    def product(block, owner, first=0):
        part = lax.dynamic_slice_in_dim(base_weight, owner * width + first, block.shape[1], axis=0)
        return jnp.dot(block, part, preferred_element_type=F32)

    mate = send(own, SWAP)
    left = own[:, :half]
    mid = [send(left, ACROSS)]
    partial = shrink(inputs, shrink_table, adapter_ids)
    right = after(own, partial)[:, half:]
    mid.append(send(right, ACROSS))
    mate_partial = send(partial, INWARD)
    total = product(own, here)

    mid_out = [send(after(mid[0], total), OUTWARD)]
    end = [send(after(left, mid[0], total), FAR), send(after(right, mid[1]), FAR)]
    mate, mate_partial = lax.optimization_barrier((mate, mate_partial, mid[1], total))[:2]
    both = send(jnp.stack([partial, mate_partial]), ACROSS)
    mid_out.append(send(mid[1], OUTWARD))
    total = total + product(mate, here ^ 1)

    end[0], both = lax.optimization_barrier((end[0], both, total))[:2]
    end_out = [send(end[0], OUTWARD)]
    shrunk = (
        partial.astype(F32) + mate_partial.astype(F32) + both[0].astype(F32) + both[1].astype(F32)
    ).astype(BF16)
    shrunk = jnp.where(is_end, send(shrunk, OUTWARD), shrunk)
    total = total + product(jnp.where(is_end, mid_out[0], mid[0]), far_mid)

    late = after(end[1], total)
    shrunk = after(shrunk, late)
    end_out += [send(late[:, : half - last], OUTWARD), send(late[:, half - last :], OUTWARD)]
    total = total + product(jnp.where(is_end, mid_out[1], mid[1]), far_mid, half)
    total = total + jnp.concatenate(expand(shrunk, expand_table, adapter_ids))
    total = total + product(jnp.where(is_end, end_out[0], end[0]), far_end)
    block = jnp.where(is_end, after(end_out[1], total), late[:, : half - last])
    total = total + product(block, far_end, half)
    block = jnp.where(is_end, after(end_out[2], total), late[:, half - last :])
    total = total + product(block, far_end, width - last)
    return total.astype(BF16).reshape(chats, span, -1)


def solution(mesh):
    n = mesh.shape["tensor"]
    return jax.shard_map(
        line if n == 4 else ring(n),
        mesh=mesh,
        in_specs=(
            P(("groups", "dp"), "seq", "tensor"),
            P(None, "tensor"),
            P("groups", "tensor", None),
            P("groups", None, "tensor"),
            P(("groups", "dp")),
        ),
        out_specs=P(("groups", "dp"), "seq", "tensor"),
        check_vma=False,
    )
```

```python
import jax
import jax.numpy as jnp
from jax import lax
from jax.sharding import PartitionSpec as P

F32, BF16 = jnp.float32, jnp.bfloat16


def shrink(inputs, shrink_table, adapter_ids):
    return jnp.concatenate(
        [
            jnp.dot(inputs[c], shrink_table[adapter_ids[c]], preferred_element_type=F32).astype(BF16)
            for c in range(inputs.shape[0])
        ]
    )


def expand(shrunk, expand_table, adapter_ids):
    chats = adapter_ids.shape[0]
    parts = shrunk.reshape(chats, -1, shrunk.shape[-1])
    return [
        jnp.dot(parts[c], expand_table[adapter_ids[c]], preferred_element_type=F32)
        for c in range(chats)
    ]


def ring(n):
    right = [(i, (i + 1) % n) for i in range(n)]
    left = [(i, (i - 1) % n) for i in range(n)]

    def local(inputs, base_weight, shrink_table, expand_table, adapter_ids):
        chats, span, width = inputs.shape
        here = lax.axis_index("tensor")
        own = inputs.reshape(chats * span, width)

        def product(block, owner, first=0):
            rows = lax.dynamic_slice_in_dim(
                base_weight, lax.rem(owner + 2 * n, n) * width + first, block.shape[1], axis=0
            )
            return jnp.dot(block, rows, preferred_element_type=F32)

        shrunk = lax.psum(shrink(inputs, shrink_table, adapter_ids), "tensor")
        total = product(own, here)
        from_left = from_right = own
        for step in range(1, (n - 1) // 2 + 1):
            from_left = lax.ppermute(from_left, "tensor", right)
            from_right = lax.ppermute(from_right, "tensor", left)
            total = total + product(from_left, here - step)
            total = total + product(from_right, here + step)
        if n > 1 and n % 2 == 0:
            half = width // 2
            one = lax.ppermute(from_left[:, :half], "tensor", right)
            two = lax.ppermute(from_right[:, half:], "tensor", left)
            total = total + product(one, here - n // 2)
            total = total + product(two, here - n // 2, half)
        total = total + jnp.concatenate(expand(shrunk, expand_table, adapter_ids))
        return total.astype(BF16).reshape(chats, span, -1)

    return local


INWARD = [(0, 1), (3, 2)]
OUTWARD = [(1, 0), (2, 3)]
ACROSS = [(1, 2), (2, 1)]
SWAP = INWARD + OUTWARD


def send(block, pairs):
    return lax.ppermute(block, "tensor", pairs)


def after(block, *earlier):
    return lax.optimization_barrier((block,) + earlier)[0]


def line(inputs, base_weight, shrink_table, expand_table, adapter_ids):
    chats, span, width = inputs.shape
    rows = chats * span
    here = lax.axis_index("tensor")
    is_end = (here == 0) | (here == 3)
    far_mid = jnp.where(here < 2, 2, 1)
    far_end = jnp.where(here < 2, 3, 0)
    own = inputs.reshape(rows, width)
    half, low = width // 2, rows // 4 * 3

    def product(block, owner, first=0):
        part = lax.dynamic_slice_in_dim(base_weight, owner * width + first, block.shape[1], axis=0)
        return jnp.dot(block, part, preferred_element_type=F32)

    mate = send(own, SWAP)
    mid = [send(own[:, :half], ACROSS)]
    partial = shrink(inputs, shrink_table, adapter_ids)
    mid.append(send(after(own, partial)[:, half:], ACROSS))
    mate_partial = send(partial, INWARD)
    total = product(own, here)

    mid_out = [send(after(mid[0], total), OUTWARD)]
    mate, mate_partial = lax.optimization_barrier((mate, mate_partial, mid[0], total))[:2]
    both = send(jnp.stack([partial, mate_partial]), ACROSS)
    first = mate[:, :half]
    end = [send(first, ACROSS)]
    end.append(send(after(mate, end[0])[:, half:], ACROSS))
    mid_out.append(send(after(mid[1], first), OUTWARD))
    total = total + product(mate, here ^ 1)

    end[0], both = lax.optimization_barrier((end[0], both, total))[:2]
    end_out = [send(end[0], OUTWARD)]
    shrunk = (
        partial.astype(F32) + mate_partial.astype(F32) + both[0].astype(F32) + both[1].astype(F32)
    ).astype(BF16)
    shrunk = jnp.where(is_end, send(shrunk, OUTWARD), shrunk)
    total = total + product(jnp.where(is_end, mid_out[0], mid[0]), far_mid)

    late = after(end[1], total)
    shrunk = after(shrunk, late)
    end_out += [send(late[:low], OUTWARD), send(late[low:], OUTWARD)]
    total = total + product(jnp.where(is_end, mid_out[1], mid[1]), far_mid, half)
    total = total + jnp.concatenate(expand(shrunk, expand_table, adapter_ids))
    total = total + product(jnp.where(is_end, end_out[0], end[0]), far_end)
    out = total.astype(BF16)
    for piece, first in ((1, 0), (2, low)):
        block = jnp.where(is_end, after(end_out[piece], out), late[first:][: end_out[piece].shape[0]])
        part = total[first:][: block.shape[0]] + product(block, far_end, half)
        out = lax.dynamic_update_slice(out, part.astype(BF16), (first, 0))
    return out.reshape(chats, span, -1)


def solution(mesh):
    n = mesh.shape["tensor"]
    return jax.shard_map(
        line if n == 4 else ring(n),
        mesh=mesh,
        in_specs=(
            P(("groups", "dp"), "seq", "tensor"),
            P(None, "tensor"),
            P("groups", "tensor", None),
            P("groups", None, "tensor"),
            P(("groups", "dp")),
        ),
        out_specs=P(("groups", "dp"), "seq", "tensor"),
        check_vma=False,
    )
```

```python
import jax
import jax.numpy as jnp
from jax import lax
from jax.sharding import PartitionSpec as P

F32, BF16 = jnp.float32, jnp.bfloat16


def shrink(inputs, shrink_table, adapter_ids):
    return jnp.concatenate(
        [
            jnp.dot(inputs[c], shrink_table[adapter_ids[c]], preferred_element_type=F32).astype(BF16)
            for c in range(inputs.shape[0])
        ]
    )


def expand(shrunk, expand_table, adapter_ids):
    chats = adapter_ids.shape[0]
    parts = shrunk.reshape(chats, -1, shrunk.shape[-1])
    return [
        jnp.dot(parts[c], expand_table[adapter_ids[c]], preferred_element_type=F32)
        for c in range(chats)
    ]


def ring(n):
    right = [(i, (i + 1) % n) for i in range(n)]
    left = [(i, (i - 1) % n) for i in range(n)]

    def local(inputs, base_weight, shrink_table, expand_table, adapter_ids):
        chats, span, width = inputs.shape
        here = lax.axis_index("tensor")
        own = inputs.reshape(chats * span, width)

        def product(block, owner, first=0):
            rows = lax.dynamic_slice_in_dim(
                base_weight, lax.rem(owner + 2 * n, n) * width + first, block.shape[1], axis=0
            )
            return jnp.dot(block, rows, preferred_element_type=F32)

        shrunk = lax.psum(shrink(inputs, shrink_table, adapter_ids), "tensor")
        total = product(own, here)
        from_left = from_right = own
        for step in range(1, (n - 1) // 2 + 1):
            from_left = lax.ppermute(from_left, "tensor", right)
            from_right = lax.ppermute(from_right, "tensor", left)
            total = total + product(from_left, here - step)
            total = total + product(from_right, here + step)
        if n > 1 and n % 2 == 0:
            half = width // 2
            one = lax.ppermute(from_left[:, :half], "tensor", right)
            two = lax.ppermute(from_right[:, half:], "tensor", left)
            total = total + product(one, here - n // 2)
            total = total + product(two, here - n // 2, half)
        total = total + jnp.concatenate(expand(shrunk, expand_table, adapter_ids))
        return total.astype(BF16).reshape(chats, span, -1)

    return local


INWARD = [(0, 1), (3, 2)]
OUTWARD = [(1, 0), (2, 3)]
ACROSS = [(1, 2), (2, 1)]
SWAP = INWARD + OUTWARD


def send(block, pairs):
    return lax.ppermute(block, "tensor", pairs)


def after(block, *earlier):
    return lax.optimization_barrier((block,) + earlier)[0]


def line(inputs, base_weight, shrink_table, expand_table, adapter_ids):
    chats, span, width = inputs.shape
    rows = chats * span
    here = lax.axis_index("tensor")
    is_end = (here == 0) | (here == 3)
    far_mid = jnp.where(here < 2, 2, 1)
    far_end = jnp.where(here < 2, 3, 0)
    own = inputs.reshape(rows, width)
    half, last = width // 2, width // 8

    def product(block, owner, first=0):
        part = lax.dynamic_slice_in_dim(base_weight, owner * width + first, block.shape[1], axis=0)
        return jnp.dot(block, part, preferred_element_type=F32)

    mate = send(own, SWAP)
    mid = [send(own[:, :half], ACROSS)]
    partial = shrink(inputs, shrink_table, adapter_ids)
    mid.append(send(after(own, partial)[:, half:], ACROSS))
    mate_partial = send(partial, INWARD)
    total = product(own, here)

    mid_out = [send(after(mid[0], total), OUTWARD)]
    mate, mate_partial = lax.optimization_barrier((mate, mate_partial, mid[0], total))[:2]
    both = send(jnp.stack([partial, mate_partial]), ACROSS)
    first = mate[:, :half]
    end = [send(first, ACROSS)]
    end.append(send(after(mate, end[0])[:, half:], ACROSS))
    mid_out.append(send(after(mid[1], first), OUTWARD))
    total = total + product(mate, here ^ 1)

    end[0], both = lax.optimization_barrier((end[0], both, total))[:2]
    end_out = [send(end[0], OUTWARD)]
    shrunk = (
        partial.astype(F32) + mate_partial.astype(F32) + both[0].astype(F32) + both[1].astype(F32)
    ).astype(BF16)
    shrunk = jnp.where(is_end, send(shrunk, OUTWARD), shrunk)
    total = total + product(jnp.where(is_end, mid_out[0], mid[0]), far_mid)

    late = after(end[1], total)
    last_rows = after(
        lax.dynamic_slice_in_dim(base_weight, (far_end + 1) * width - last, last, axis=0), late
    )
    shrunk = after(shrunk, late)
    end_out += [send(late[:, : half - last], OUTWARD), send(late[:, half - last :], OUTWARD)]
    total = total + product(jnp.where(is_end, mid_out[1], mid[1]), far_mid, half)
    total = total + jnp.concatenate(expand(shrunk, expand_table, adapter_ids))
    total = total + product(jnp.where(is_end, end_out[0], end[0]), far_end)
    block = jnp.where(is_end, after(end_out[1], total), late[:, : half - last])
    total = total + product(block, far_end, half)
    block = jnp.where(is_end, after(end_out[2], total), late[:, half - last :])
    total = total + jnp.dot(block, last_rows, preferred_element_type=F32)
    return total.astype(BF16).reshape(chats, span, -1)


def solution(mesh):
    n = mesh.shape["tensor"]
    return jax.shard_map(
        line if n == 4 else ring(n),
        mesh=mesh,
        in_specs=(
            P(("groups", "dp"), "seq", "tensor"),
            P(None, "tensor"),
            P("groups", "tensor", None),
            P("groups", None, "tensor"),
            P(("groups", "dp")),
        ),
        out_specs=P(("groups", "dp"), "seq", "tensor"),
        check_vma=False,
    )
```

```python
import jax
import jax.numpy as jnp
from jax import lax
from jax.sharding import PartitionSpec as P

F32, BF16 = jnp.float32, jnp.bfloat16


def shrink(inputs, shrink_table, adapter_ids):
    return jnp.concatenate(
        [
            jnp.dot(inputs[c], shrink_table[adapter_ids[c]], preferred_element_type=F32).astype(BF16)
            for c in range(inputs.shape[0])
        ]
    )


def expand(shrunk, expand_table, adapter_ids):
    chats = adapter_ids.shape[0]
    parts = shrunk.reshape(chats, -1, shrunk.shape[-1])
    return [
        jnp.dot(parts[c], expand_table[adapter_ids[c]], preferred_element_type=F32)
        for c in range(chats)
    ]


def ring(n):
    right = [(i, (i + 1) % n) for i in range(n)]
    left = [(i, (i - 1) % n) for i in range(n)]

    def local(inputs, base_weight, shrink_table, expand_table, adapter_ids):
        chats, span, width = inputs.shape
        here = lax.axis_index("tensor")
        own = inputs.reshape(chats * span, width)

        def product(block, owner, first=0):
            rows = lax.dynamic_slice_in_dim(
                base_weight, lax.rem(owner + 2 * n, n) * width + first, block.shape[1], axis=0
            )
            return jnp.dot(block, rows, preferred_element_type=F32)

        shrunk = lax.psum(shrink(inputs, shrink_table, adapter_ids), "tensor")
        total = product(own, here)
        from_left = from_right = own
        for step in range(1, (n - 1) // 2 + 1):
            from_left = lax.ppermute(from_left, "tensor", right)
            from_right = lax.ppermute(from_right, "tensor", left)
            total = total + product(from_left, here - step)
            total = total + product(from_right, here + step)
        if n > 1 and n % 2 == 0:
            half = width // 2
            one = lax.ppermute(from_left[:, :half], "tensor", right)
            two = lax.ppermute(from_right[:, half:], "tensor", left)
            total = total + product(one, here - n // 2)
            total = total + product(two, here - n // 2, half)
        total = total + jnp.concatenate(expand(shrunk, expand_table, adapter_ids))
        return total.astype(BF16).reshape(chats, span, -1)

    return local


INWARD = [(0, 1), (3, 2)]
OUTWARD = [(1, 0), (2, 3)]
ACROSS = [(1, 2), (2, 1)]
SWAP = INWARD + OUTWARD


def send(block, pairs):
    return lax.ppermute(block, "tensor", pairs)


def after(block, *earlier):
    return lax.optimization_barrier((block,) + earlier)[0]


def line(inputs, base_weight, shrink_table, expand_table, adapter_ids):
    chats, span, width = inputs.shape
    rows = chats * span
    here = lax.axis_index("tensor")
    is_end = (here == 0) | (here == 3)
    far_mid = jnp.where(here < 2, 2, 1)
    far_end = jnp.where(here < 2, 3, 0)
    own = inputs.reshape(rows, width)
    half, last = width // 2, width // 8

    def product(block, owner, first=0):
        part = lax.dynamic_slice_in_dim(base_weight, owner * width + first, block.shape[1], axis=0)
        return jnp.dot(block, part, preferred_element_type=F32)

    mate = send(own, SWAP)
    mid = [send(own[:, :half], ACROSS)]
    partial = shrink(inputs, shrink_table, adapter_ids)
    mid.append(send(after(own, partial)[:, half:], ACROSS))
    mate_partial = send(partial, INWARD)
    total = product(own, here)

    mid_out = [send(after(mid[0], total), OUTWARD)]
    mate, mate_partial = lax.optimization_barrier((mate, mate_partial, mid[0], total))[:2]
    both = send(jnp.stack([partial, mate_partial]), ACROSS)
    first = mate[:, :half]
    end = [send(first, ACROSS)]
    end.append(send(after(mate, end[0])[:, half:], ACROSS))
    mid_out.append(send(after(mid[1], first), OUTWARD))
    total = total + product(mate, here ^ 1)

    end[0], both = lax.optimization_barrier((end[0], both, total))[:2]
    end_out = [send(end[0], OUTWARD)]
    shrunk = (
        partial.astype(F32) + mate_partial.astype(F32) + both[0].astype(F32) + both[1].astype(F32)
    ).astype(BF16)
    shrunk = jnp.where(is_end, send(shrunk, OUTWARD), shrunk)
    total = total + product(jnp.where(is_end, mid_out[0], mid[0]), far_mid)

    late = after(end[1], total)
    begin = (after(far_end, late) + 1) * width - last
    last_rows = lax.dynamic_slice_in_dim(base_weight, begin, last, axis=0)
    shrunk = after(shrunk, late)
    end_out += [send(late[:, : half - last], OUTWARD), send(late[:, half - last :], OUTWARD)]
    total = total + product(jnp.where(is_end, mid_out[1], mid[1]), far_mid, half)
    total = total + jnp.concatenate(expand(shrunk, expand_table, adapter_ids))
    end_out[0], last_rows = lax.optimization_barrier((end_out[0], last_rows))
    total = total + product(jnp.where(is_end, end_out[0], end[0]), far_end)
    block = jnp.where(is_end, after(end_out[1], total), late[:, : half - last])
    total = total + product(block, far_end, half)
    block = jnp.where(is_end, after(end_out[2], total), late[:, half - last :])
    total = total + jnp.dot(block, last_rows, preferred_element_type=F32)
    return total.astype(BF16).reshape(chats, span, -1)


def solution(mesh):
    n = mesh.shape["tensor"]
    return jax.shard_map(
        line if n == 4 else ring(n),
        mesh=mesh,
        in_specs=(
            P(("groups", "dp"), "seq", "tensor"),
            P(None, "tensor"),
            P("groups", "tensor", None),
            P("groups", None, "tensor"),
            P(("groups", "dp")),
        ),
        out_specs=P(("groups", "dp"), "seq", "tensor"),
        check_vma=False,
    )
```

```python
import jax
import jax.numpy as jnp
from jax import lax
from jax.sharding import PartitionSpec as P

F32, BF16 = jnp.float32, jnp.bfloat16


def shrink(inputs, shrink_table, adapter_ids):
    return jnp.concatenate(
        [
            jnp.dot(inputs[c], shrink_table[adapter_ids[c]], preferred_element_type=F32).astype(BF16)
            for c in range(inputs.shape[0])
        ]
    )


def expand(shrunk, expand_table, adapter_ids):
    chats = adapter_ids.shape[0]
    parts = shrunk.reshape(chats, -1, shrunk.shape[-1])
    return [
        jnp.dot(parts[c], expand_table[adapter_ids[c]], preferred_element_type=F32)
        for c in range(chats)
    ]


def ring(n):
    right = [(i, (i + 1) % n) for i in range(n)]
    left = [(i, (i - 1) % n) for i in range(n)]

    def local(inputs, base_weight, shrink_table, expand_table, adapter_ids):
        chats, span, width = inputs.shape
        here = lax.axis_index("tensor")
        own = inputs.reshape(chats * span, width)

        def product(block, owner, first=0):
            rows = lax.dynamic_slice_in_dim(
                base_weight, lax.rem(owner + 2 * n, n) * width + first, block.shape[1], axis=0
            )
            return jnp.dot(block, rows, preferred_element_type=F32)

        shrunk = lax.psum(shrink(inputs, shrink_table, adapter_ids), "tensor")
        total = product(own, here)
        from_left = from_right = own
        for step in range(1, (n - 1) // 2 + 1):
            from_left = lax.ppermute(from_left, "tensor", right)
            from_right = lax.ppermute(from_right, "tensor", left)
            total = total + product(from_left, here - step)
            total = total + product(from_right, here + step)
        if n > 1 and n % 2 == 0:
            half = width // 2
            one = lax.ppermute(from_left[:, :half], "tensor", right)
            two = lax.ppermute(from_right[:, half:], "tensor", left)
            total = total + product(one, here - n // 2)
            total = total + product(two, here - n // 2, half)
        total = total + jnp.concatenate(expand(shrunk, expand_table, adapter_ids))
        return total.astype(BF16).reshape(chats, span, -1)

    return local


INWARD = [(0, 1), (3, 2)]
OUTWARD = [(1, 0), (2, 3)]
ACROSS = [(1, 2), (2, 1)]
SWAP = INWARD + OUTWARD


def send(block, pairs):
    return lax.ppermute(block, "tensor", pairs)


def after(block, *earlier):
    return lax.optimization_barrier((block,) + earlier)[0]


def line(inputs, base_weight, shrink_table, expand_table, adapter_ids):
    chats, span, width = inputs.shape
    rows = chats * span
    here = lax.axis_index("tensor")
    is_end = (here == 0) | (here == 3)
    far_mid = jnp.where(here < 2, 2, 1)
    far_end = jnp.where(here < 2, 3, 0)
    own = inputs.reshape(rows, width)
    half, last = width // 2, width // 8

    def product(block, owner, first=0):
        part = lax.dynamic_slice_in_dim(base_weight, owner * width + first, block.shape[1], axis=0)
        return jnp.dot(block, part, preferred_element_type=F32)

    mate = send(own, SWAP)
    mid = [send(own[:, :half], ACROSS)]
    partial = shrink(inputs, shrink_table, adapter_ids)
    mid.append(send(after(own, partial)[:, half:], ACROSS))
    mate_partial = send(partial, INWARD)
    total = product(own, here)

    mid_out = [send(after(mid[0], total), OUTWARD)]
    mate, mate_partial = lax.optimization_barrier((mate, mate_partial, mid[0], total))[:2]
    both = send(jnp.stack([partial, mate_partial]), ACROSS)
    first = mate[:, :half]
    end = [send(first, ACROSS)]
    end.append(send(after(mate, end[0])[:, half:], ACROSS))
    mid_out.append(send(after(mid[1], first), OUTWARD))
    total = total + product(mate, here ^ 1)

    end[0], both = lax.optimization_barrier((end[0], both, total))[:2]
    end_out = [send(end[0], OUTWARD)]
    shrunk = (
        partial.astype(F32) + mate_partial.astype(F32) + both[0].astype(F32) + both[1].astype(F32)
    ).astype(BF16)
    shrunk = jnp.where(is_end, send(shrunk, OUTWARD), shrunk)
    total = total + product(jnp.where(is_end, mid_out[0], mid[0]), far_mid)

    late = after(end[1], total)
    begin = (after(far_end, late) + 1) * width - last
    last_rows = lax.dynamic_slice_in_dim(base_weight, begin, last, axis=0)
    late, last_rows = lax.optimization_barrier((late, last_rows))
    shrunk = after(shrunk, late)
    end_out += [send(late[:, : half - last], OUTWARD), send(late[:, half - last :], OUTWARD)]
    total = total + product(jnp.where(is_end, mid_out[1], mid[1]), far_mid, half)
    total = total + jnp.concatenate(expand(shrunk, expand_table, adapter_ids))
    total = total + product(jnp.where(is_end, end_out[0], end[0]), far_end)
    block = jnp.where(is_end, after(end_out[1], total), late[:, : half - last])
    total = total + product(block, far_end, half)
    block = jnp.where(is_end, after(end_out[2], total), late[:, half - last :])
    total = total + jnp.dot(block, last_rows, preferred_element_type=F32)
    return total.astype(BF16).reshape(chats, span, -1)


def solution(mesh):
    n = mesh.shape["tensor"]
    return jax.shard_map(
        line if n == 4 else ring(n),
        mesh=mesh,
        in_specs=(
            P(("groups", "dp"), "seq", "tensor"),
            P(None, "tensor"),
            P("groups", "tensor", None),
            P("groups", None, "tensor"),
            P(("groups", "dp")),
        ),
        out_specs=P(("groups", "dp"), "seq", "tensor"),
        check_vma=False,
    )
```

```python
import jax
import jax.numpy as jnp
from jax import lax
from jax.sharding import PartitionSpec as P

F32, BF16 = jnp.float32, jnp.bfloat16


def shrink(inputs, shrink_table, adapter_ids):
    return jnp.concatenate(
        [
            jnp.dot(inputs[c], shrink_table[adapter_ids[c]], preferred_element_type=F32).astype(BF16)
            for c in range(inputs.shape[0])
        ]
    )


def expand(shrunk, expand_table, adapter_ids):
    chats = adapter_ids.shape[0]
    parts = shrunk.reshape(chats, -1, shrunk.shape[-1])
    return [
        jnp.dot(parts[c], expand_table[adapter_ids[c]], preferred_element_type=F32)
        for c in range(chats)
    ]


def ring(n):
    right = [(i, (i + 1) % n) for i in range(n)]
    left = [(i, (i - 1) % n) for i in range(n)]

    def local(inputs, base_weight, shrink_table, expand_table, adapter_ids):
        chats, span, width = inputs.shape
        here = lax.axis_index("tensor")
        own = inputs.reshape(chats * span, width)

        def product(block, owner, first=0):
            rows = lax.dynamic_slice_in_dim(
                base_weight, lax.rem(owner + 2 * n, n) * width + first, block.shape[1], axis=0
            )
            return jnp.dot(block, rows, preferred_element_type=F32)

        shrunk = lax.psum(shrink(inputs, shrink_table, adapter_ids), "tensor")
        total = product(own, here)
        from_left = from_right = own
        for step in range(1, (n - 1) // 2 + 1):
            from_left = lax.ppermute(from_left, "tensor", right)
            from_right = lax.ppermute(from_right, "tensor", left)
            total = total + product(from_left, here - step)
            total = total + product(from_right, here + step)
        if n > 1 and n % 2 == 0:
            half = width // 2
            one = lax.ppermute(from_left[:, :half], "tensor", right)
            two = lax.ppermute(from_right[:, half:], "tensor", left)
            total = total + product(one, here - n // 2)
            total = total + product(two, here - n // 2, half)
        total = total + jnp.concatenate(expand(shrunk, expand_table, adapter_ids))
        return total.astype(BF16).reshape(chats, span, -1)

    return local


INWARD = [(0, 1), (3, 2)]
OUTWARD = [(1, 0), (2, 3)]
ACROSS = [(1, 2), (2, 1)]
SWAP = INWARD + OUTWARD


def send(block, pairs):
    return lax.ppermute(block, "tensor", pairs)


def after(block, *earlier):
    return lax.optimization_barrier((block,) + earlier)[0]


def line(inputs, base_weight, shrink_table, expand_table, adapter_ids):
    chats, span, width = inputs.shape
    rows = chats * span
    here = lax.axis_index("tensor")
    is_end = (here == 0) | (here == 3)
    far_mid = jnp.where(here < 2, 2, 1)
    far_end = jnp.where(here < 2, 3, 0)
    own = inputs.reshape(rows, width)
    half, last = width // 2, width // 8

    def product(block, owner, first=0):
        part = lax.dynamic_slice_in_dim(base_weight, owner * width + first, block.shape[1], axis=0)
        return jnp.dot(block, part, preferred_element_type=F32)

    mate = send(own, SWAP)
    mid = [send(own[:, :half], ACROSS)]
    partial = shrink(inputs, shrink_table, adapter_ids)
    mid.append(send(after(own, partial)[:, half:], ACROSS))
    mate_partial = send(partial, INWARD)
    total = product(own, here)

    mid_out = [send(after(mid[0], total), OUTWARD)]
    mate, mate_partial = lax.optimization_barrier((mate, mate_partial, mid[0], total))[:2]
    both = send(jnp.stack([partial, mate_partial]), ACROSS)
    first = mate[:, :half]
    end = [send(first, ACROSS)]
    end.append(send(after(mate, end[0])[:, half:], ACROSS))
    mid_out.append(send(after(mid[1], first), OUTWARD))
    total = total + product(mate, here ^ 1)

    end[0], both = lax.optimization_barrier((end[0], both, total))[:2]
    end_out = [send(end[0], OUTWARD)]
    shrunk = (
        partial.astype(F32) + mate_partial.astype(F32) + both[0].astype(F32) + both[1].astype(F32)
    ).astype(BF16)
    shrunk = jnp.where(is_end, send(shrunk, OUTWARD), shrunk)

    late = after(end[1], total)
    begin = (after(far_end, late) + 1) * width - last
    last_rows = lax.dynamic_slice_in_dim(base_weight, begin, last, axis=0)
    late, last_rows = lax.optimization_barrier((late, last_rows))
    mid_out[0], shrunk = lax.optimization_barrier((mid_out[0], shrunk, late))[:2]
    end_out += [send(late[:, : half - last], OUTWARD), send(late[:, half - last :], OUTWARD)]
    total = total + product(jnp.where(is_end, mid_out[0], mid[0]), far_mid)
    total = total + product(jnp.where(is_end, mid_out[1], mid[1]), far_mid, half)
    total = total + jnp.concatenate(expand(shrunk, expand_table, adapter_ids))
    total = total + product(jnp.where(is_end, end_out[0], end[0]), far_end)
    block = jnp.where(is_end, after(end_out[1], total), late[:, : half - last])
    total = total + product(block, far_end, half)
    block = jnp.where(is_end, after(end_out[2], total), late[:, half - last :])
    total = total + jnp.dot(block, last_rows, preferred_element_type=F32)
    return total.astype(BF16).reshape(chats, span, -1)


def solution(mesh):
    n = mesh.shape["tensor"]
    return jax.shard_map(
        line if n == 4 else ring(n),
        mesh=mesh,
        in_specs=(
            P(("groups", "dp"), "seq", "tensor"),
            P(None, "tensor"),
            P("groups", "tensor", None),
            P("groups", None, "tensor"),
            P(("groups", "dp")),
        ),
        out_specs=P(("groups", "dp"), "seq", "tensor"),
        check_vma=False,
    )
```

```python
import jax
import jax.numpy as jnp
from jax import lax
from jax.sharding import PartitionSpec as P

F32, BF16 = jnp.float32, jnp.bfloat16


def shrink(inputs, shrink_table, adapter_ids):
    return jnp.concatenate(
        [
            jnp.dot(inputs[c], shrink_table[adapter_ids[c]], preferred_element_type=F32).astype(BF16)
            for c in range(inputs.shape[0])
        ]
    )


def expand(shrunk, expand_table, adapter_ids):
    chats = adapter_ids.shape[0]
    parts = shrunk.reshape(chats, -1, shrunk.shape[-1])
    return [
        jnp.dot(parts[c], expand_table[adapter_ids[c]], preferred_element_type=F32)
        for c in range(chats)
    ]


def ring(n):
    right = [(i, (i + 1) % n) for i in range(n)]
    left = [(i, (i - 1) % n) for i in range(n)]

    def local(inputs, base_weight, shrink_table, expand_table, adapter_ids):
        chats, span, width = inputs.shape
        here = lax.axis_index("tensor")
        own = inputs.reshape(chats * span, width)

        def product(block, owner, first=0):
            rows = lax.dynamic_slice_in_dim(
                base_weight, lax.rem(owner + 2 * n, n) * width + first, block.shape[1], axis=0
            )
            return jnp.dot(block, rows, preferred_element_type=F32)

        shrunk = lax.psum(shrink(inputs, shrink_table, adapter_ids), "tensor")
        total = product(own, here)
        from_left = from_right = own
        for step in range(1, (n - 1) // 2 + 1):
            from_left = lax.ppermute(from_left, "tensor", right)
            from_right = lax.ppermute(from_right, "tensor", left)
            total = total + product(from_left, here - step)
            total = total + product(from_right, here + step)
        if n > 1 and n % 2 == 0:
            half = width // 2
            one = lax.ppermute(from_left[:, :half], "tensor", right)
            two = lax.ppermute(from_right[:, half:], "tensor", left)
            total = total + product(one, here - n // 2)
            total = total + product(two, here - n // 2, half)
        total = total + jnp.concatenate(expand(shrunk, expand_table, adapter_ids))
        return total.astype(BF16).reshape(chats, span, -1)

    return local


INWARD = [(0, 1), (3, 2)]
OUTWARD = [(1, 0), (2, 3)]
ACROSS = [(1, 2), (2, 1)]
SWAP = INWARD + OUTWARD


def send(block, pairs):
    return lax.ppermute(block, "tensor", pairs)


def after(block, *earlier):
    return lax.optimization_barrier((block,) + earlier)[0]


def line(inputs, base_weight, shrink_table, expand_table, adapter_ids):
    chats, span, width = inputs.shape
    rows = chats * span
    here = lax.axis_index("tensor")
    is_end = (here == 0) | (here == 3)
    far_mid = jnp.where(here < 2, 2, 1)
    far_end = jnp.where(here < 2, 3, 0)
    own = inputs.reshape(rows, width)
    half, last = width // 2, width // 8

    def product(block, owner, first=0):
        part = lax.dynamic_slice_in_dim(base_weight, owner * width + first, block.shape[1], axis=0)
        return jnp.dot(block, part, preferred_element_type=F32)

    mate = send(own, SWAP)
    mid = [send(own[:, :half], ACROSS)]
    partial = shrink(inputs, shrink_table, adapter_ids)
    mid.append(send(after(own, partial)[:, half:], ACROSS))
    mate_partial = send(partial, INWARD)
    total = product(own, here)

    mid_out = [send(after(mid[0], total), OUTWARD)]
    mate, mate_partial = lax.optimization_barrier((mate, mate_partial, mid[0], total))[:2]
    both = send(jnp.stack([partial, mate_partial]), ACROSS)
    first = mate[:, :half]
    end = [send(first, ACROSS)]
    end.append(send(after(mate, end[0])[:, half:], ACROSS))
    mid_out.append(send(after(mid[1], first), OUTWARD))
    total = total + product(mate, here ^ 1)

    end[0], both = lax.optimization_barrier((end[0], both, total))[:2]
    end_out = [send(end[0], OUTWARD)]
    shrunk = (
        partial.astype(F32) + mate_partial.astype(F32) + both[0].astype(F32) + both[1].astype(F32)
    ).astype(BF16)
    total = total + product(jnp.where(is_end, mid_out[0], mid[0]), far_mid)

    late = after(end[1], total)
    begin = (after(far_end, late) + 1) * width - last
    last_rows = lax.dynamic_slice_in_dim(base_weight, begin, last, axis=0)
    late, last_rows = lax.optimization_barrier((late, last_rows))
    shrunk = after(shrunk, late)
    shrunk = jnp.where(is_end, send(shrunk, OUTWARD), shrunk)
    end_out += [send(late[:, : half - last], OUTWARD), send(late[:, half - last :], OUTWARD)]
    total = total + product(jnp.where(is_end, mid_out[1], mid[1]), far_mid, half)
    total = total + jnp.concatenate(expand(shrunk, expand_table, adapter_ids))
    total = total + product(jnp.where(is_end, end_out[0], end[0]), far_end)
    block = jnp.where(is_end, after(end_out[1], total), late[:, : half - last])
    total = total + product(block, far_end, half)
    block = jnp.where(is_end, after(end_out[2], total), late[:, half - last :])
    total = total + jnp.dot(block, last_rows, preferred_element_type=F32)
    return total.astype(BF16).reshape(chats, span, -1)


def solution(mesh):
    n = mesh.shape["tensor"]
    return jax.shard_map(
        line if n == 4 else ring(n),
        mesh=mesh,
        in_specs=(
            P(("groups", "dp"), "seq", "tensor"),
            P(None, "tensor"),
            P("groups", "tensor", None),
            P("groups", None, "tensor"),
            P(("groups", "dp")),
        ),
        out_specs=P(("groups", "dp"), "seq", "tensor"),
        check_vma=False,
    )
```

```python
import jax
import jax.numpy as jnp
from jax import lax
from jax.sharding import PartitionSpec as P

F32, BF16 = jnp.float32, jnp.bfloat16


def shrink(inputs, shrink_table, adapter_ids):
    return jnp.concatenate(
        [
            jnp.dot(inputs[c], shrink_table[adapter_ids[c]], preferred_element_type=F32).astype(BF16)
            for c in range(inputs.shape[0])
        ]
    )


def expand(shrunk, expand_table, adapter_ids):
    chats = adapter_ids.shape[0]
    parts = shrunk.reshape(chats, -1, shrunk.shape[-1])
    return [
        jnp.dot(parts[c], expand_table[adapter_ids[c]], preferred_element_type=F32)
        for c in range(chats)
    ]


def ring(n):
    right = [(i, (i + 1) % n) for i in range(n)]
    left = [(i, (i - 1) % n) for i in range(n)]

    def local(inputs, base_weight, shrink_table, expand_table, adapter_ids):
        chats, span, width = inputs.shape
        here = lax.axis_index("tensor")
        own = inputs.reshape(chats * span, width)

        def product(block, owner, first=0):
            rows = lax.dynamic_slice_in_dim(
                base_weight, lax.rem(owner + 2 * n, n) * width + first, block.shape[1], axis=0
            )
            return jnp.dot(block, rows, preferred_element_type=F32)

        shrunk = lax.psum(shrink(inputs, shrink_table, adapter_ids), "tensor")
        total = product(own, here)
        from_left = from_right = own
        for step in range(1, (n - 1) // 2 + 1):
            from_left = lax.ppermute(from_left, "tensor", right)
            from_right = lax.ppermute(from_right, "tensor", left)
            total = total + product(from_left, here - step)
            total = total + product(from_right, here + step)
        if n > 1 and n % 2 == 0:
            half = width // 2
            one = lax.ppermute(from_left[:, :half], "tensor", right)
            two = lax.ppermute(from_right[:, half:], "tensor", left)
            total = total + product(one, here - n // 2)
            total = total + product(two, here - n // 2, half)
        total = total + jnp.concatenate(expand(shrunk, expand_table, adapter_ids))
        return total.astype(BF16).reshape(chats, span, -1)

    return local


INWARD = [(0, 1), (3, 2)]
OUTWARD = [(1, 0), (2, 3)]
ACROSS = [(1, 2), (2, 1)]
SWAP = INWARD + OUTWARD


def send(block, pairs):
    return lax.ppermute(block, "tensor", pairs)


def after(block, *earlier):
    return lax.optimization_barrier((block,) + earlier)[0]


def line(inputs, base_weight, shrink_table, expand_table, adapter_ids):
    chats, span, width = inputs.shape
    rows = chats * span
    here = lax.axis_index("tensor")
    is_end = (here == 0) | (here == 3)
    far_mid = jnp.where(here < 2, 2, 1)
    far_end = jnp.where(here < 2, 3, 0)
    own = inputs.reshape(rows, width)
    half, cut, last = width // 2, width // 16 * 7, width // 8

    def product(block, owner, first=0):
        part = lax.dynamic_slice_in_dim(base_weight, owner * width + first, block.shape[1], axis=0)
        return jnp.dot(block, part, preferred_element_type=F32)

    mate = send(own, SWAP)
    mid = [send(own[:, :half], ACROSS)]
    partial = shrink(inputs, shrink_table, adapter_ids)
    mid.append(send(after(own, partial)[:, half:], ACROSS))
    mate_partial = send(partial, INWARD)
    total = product(own, here)

    mid_out = [send(after(mid[0], total), OUTWARD)]
    mate, mate_partial = lax.optimization_barrier((mate, mate_partial, mid[0], total))[:2]
    both = send(jnp.stack([partial, mate_partial]), ACROSS)
    first = mate[:, :cut]
    end = [send(first, ACROSS)]
    end.append(send(after(mate, end[0])[:, cut:], ACROSS))
    mid_out.append(send(after(mid[1], first), OUTWARD))
    total = total + product(mate, here ^ 1)

    end[0], both = lax.optimization_barrier((end[0], both, total))[:2]
    end_out = [send(end[0], OUTWARD)]
    shrunk = (
        partial.astype(F32) + mate_partial.astype(F32) + both[0].astype(F32) + both[1].astype(F32)
    ).astype(BF16)
    shrunk = jnp.where(is_end, send(shrunk, OUTWARD), shrunk)
    total = total + product(jnp.where(is_end, mid_out[0], mid[0]), far_mid)

    late = after(end[1], total)
    begin = (after(far_end, late) + 1) * width - last
    last_rows = lax.dynamic_slice_in_dim(base_weight, begin, last, axis=0)
    late, last_rows = lax.optimization_barrier((late, last_rows))
    shrunk = after(shrunk, late)
    end_out += [send(late[:, :-last], OUTWARD), send(late[:, -last:], OUTWARD)]
    total = total + product(jnp.where(is_end, mid_out[1], mid[1]), far_mid, half)
    total = total + jnp.concatenate(expand(shrunk, expand_table, adapter_ids))
    total = total + product(jnp.where(is_end, end_out[0], end[0]), far_end)
    block = jnp.where(is_end, after(end_out[1], total), late[:, :-last])
    total = total + product(block, far_end, cut)
    block = jnp.where(is_end, after(end_out[2], total), late[:, -last:])
    total = total + jnp.dot(block, last_rows, preferred_element_type=F32)
    return total.astype(BF16).reshape(chats, span, -1)


def solution(mesh):
    n = mesh.shape["tensor"]
    return jax.shard_map(
        line if n == 4 else ring(n),
        mesh=mesh,
        in_specs=(
            P(("groups", "dp"), "seq", "tensor"),
            P(None, "tensor"),
            P("groups", "tensor", None),
            P("groups", None, "tensor"),
            P(("groups", "dp")),
        ),
        out_specs=P(("groups", "dp"), "seq", "tensor"),
        check_vma=False,
    )
```

```python
import jax
import jax.numpy as jnp
from jax import lax
from jax.sharding import PartitionSpec as P

F32, BF16 = jnp.float32, jnp.bfloat16


def shrink(inputs, shrink_table, adapter_ids):
    return jnp.concatenate(
        [
            jnp.dot(inputs[c], shrink_table[adapter_ids[c]], preferred_element_type=F32).astype(BF16)
            for c in range(inputs.shape[0])
        ]
    )


def expand(shrunk, expand_table, adapter_ids):
    chats = adapter_ids.shape[0]
    parts = shrunk.reshape(chats, -1, shrunk.shape[-1])
    return [
        jnp.dot(parts[c], expand_table[adapter_ids[c]], preferred_element_type=F32)
        for c in range(chats)
    ]


def ring(n):
    right = [(i, (i + 1) % n) for i in range(n)]
    left = [(i, (i - 1) % n) for i in range(n)]

    def local(inputs, base_weight, shrink_table, expand_table, adapter_ids):
        chats, span, width = inputs.shape
        here = lax.axis_index("tensor")
        own = inputs.reshape(chats * span, width)

        def product(block, owner, first=0):
            rows = lax.dynamic_slice_in_dim(
                base_weight, lax.rem(owner + 2 * n, n) * width + first, block.shape[1], axis=0
            )
            return jnp.dot(block, rows, preferred_element_type=F32)

        shrunk = lax.psum(shrink(inputs, shrink_table, adapter_ids), "tensor")
        total = product(own, here)
        from_left = from_right = own
        for step in range(1, (n - 1) // 2 + 1):
            from_left = lax.ppermute(from_left, "tensor", right)
            from_right = lax.ppermute(from_right, "tensor", left)
            total = total + product(from_left, here - step)
            total = total + product(from_right, here + step)
        if n > 1 and n % 2 == 0:
            half = width // 2
            one = lax.ppermute(from_left[:, :half], "tensor", right)
            two = lax.ppermute(from_right[:, half:], "tensor", left)
            total = total + product(one, here - n // 2)
            total = total + product(two, here - n // 2, half)
        total = total + jnp.concatenate(expand(shrunk, expand_table, adapter_ids))
        return total.astype(BF16).reshape(chats, span, -1)

    return local


INWARD = [(0, 1), (3, 2)]
OUTWARD = [(1, 0), (2, 3)]
ACROSS = [(1, 2), (2, 1)]
SWAP = INWARD + OUTWARD


def send(block, pairs):
    return lax.ppermute(block, "tensor", pairs)


def after(block, *earlier):
    return lax.optimization_barrier((block,) + earlier)[0]


def line(inputs, base_weight, shrink_table, expand_table, adapter_ids):
    chats, span, width = inputs.shape
    rows = chats * span
    here = lax.axis_index("tensor")
    is_end = (here == 0) | (here == 3)
    far_mid = jnp.where(here < 2, 2, 1)
    far_end = jnp.where(here < 2, 3, 0)
    own = inputs.reshape(rows, width)
    half, last = width // 2, width // 8

    def product(block, owner, first=0):
        part = lax.dynamic_slice_in_dim(base_weight, owner * width + first, block.shape[1], axis=0)
        return jnp.dot(block, part, preferred_element_type=F32)

    mate = send(own, SWAP)
    mid = [send(own[:, :half], ACROSS)]
    partial = shrink(inputs, shrink_table, adapter_ids)
    mid.append(send(after(own, partial)[:, half:], ACROSS))
    mate_partial = send(partial, INWARD)
    total = product(own, here)

    mid_out = [send(after(mid[0], total), OUTWARD)]
    mate, mate_partial = lax.optimization_barrier((mate, mate_partial, mid[0], total))[:2]
    both = send(jnp.stack([partial, mate_partial]), ACROSS)
    first = mate[:, :half]
    end = [send(first, ACROSS)]
    end.append(send(after(mate, end[0])[:, half:], ACROSS))
    mid_out.append(send(after(mid[1], first), OUTWARD))
    total = total + product(mate, here ^ 1)

    end[0], both = lax.optimization_barrier((end[0], both, total))[:2]
    shrunk = (
        partial.astype(F32) + mate_partial.astype(F32) + both[0].astype(F32) + both[1].astype(F32)
    ).astype(BF16)
    rider = shrunk.reshape(-1, half)
    end_out = [send(jnp.concatenate([end[0], rider]), OUTWARD)]
    total = total + product(jnp.where(is_end, mid_out[0], mid[0]), far_mid)

    late = after(end[1], total)
    begin = (after(far_end, late) + 1) * width - last
    last_rows = lax.dynamic_slice_in_dim(base_weight, begin, last, axis=0)
    late, last_rows = lax.optimization_barrier((late, last_rows))
    end_out += [send(late[:, : half - last], OUTWARD), send(late[:, half - last :], OUTWARD)]
    total = total + product(jnp.where(is_end, mid_out[1], mid[1]), far_mid, half)
    ridden = end_out[0]
    shrunk = jnp.where(is_end, ridden[rows:].reshape(shrunk.shape), shrunk)
    total = total + jnp.concatenate(expand(shrunk, expand_table, adapter_ids))
    total = total + product(jnp.where(is_end, ridden[:rows], end[0]), far_end)
    block = jnp.where(is_end, after(end_out[1], total), late[:, : half - last])
    total = total + product(block, far_end, half)
    block = jnp.where(is_end, after(end_out[2], total), late[:, half - last :])
    total = total + jnp.dot(block, last_rows, preferred_element_type=F32)
    return total.astype(BF16).reshape(chats, span, -1)


def solution(mesh):
    n = mesh.shape["tensor"]
    return jax.shard_map(
        line if n == 4 else ring(n),
        mesh=mesh,
        in_specs=(
            P(("groups", "dp"), "seq", "tensor"),
            P(None, "tensor"),
            P("groups", "tensor", None),
            P("groups", None, "tensor"),
            P(("groups", "dp")),
        ),
        out_specs=P(("groups", "dp"), "seq", "tensor"),
        check_vma=False,
    )
```

```python
import jax
import jax.numpy as jnp
from jax import lax
from jax.sharding import PartitionSpec as P

F32, BF16 = jnp.float32, jnp.bfloat16


def shrink(inputs, shrink_table, adapter_ids):
    return jnp.concatenate(
        [
            jnp.dot(inputs[c], shrink_table[adapter_ids[c]], preferred_element_type=F32).astype(BF16)
            for c in range(inputs.shape[0])
        ]
    )


def expand(shrunk, expand_table, adapter_ids):
    chats = adapter_ids.shape[0]
    parts = shrunk.reshape(chats, -1, shrunk.shape[-1])
    return [
        jnp.dot(parts[c], expand_table[adapter_ids[c]], preferred_element_type=F32)
        for c in range(chats)
    ]


def ring(n):
    right = [(i, (i + 1) % n) for i in range(n)]
    left = [(i, (i - 1) % n) for i in range(n)]

    def local(inputs, base_weight, shrink_table, expand_table, adapter_ids):
        chats, span, width = inputs.shape
        here = lax.axis_index("tensor")
        own = inputs.reshape(chats * span, width)

        def product(block, owner, first=0):
            rows = lax.dynamic_slice_in_dim(
                base_weight, lax.rem(owner + 2 * n, n) * width + first, block.shape[1], axis=0
            )
            return jnp.dot(block, rows, preferred_element_type=F32)

        shrunk = lax.psum(shrink(inputs, shrink_table, adapter_ids), "tensor")
        total = product(own, here)
        from_left = from_right = own
        for step in range(1, (n - 1) // 2 + 1):
            from_left = lax.ppermute(from_left, "tensor", right)
            from_right = lax.ppermute(from_right, "tensor", left)
            total = total + product(from_left, here - step)
            total = total + product(from_right, here + step)
        if n > 1 and n % 2 == 0:
            half = width // 2
            one = lax.ppermute(from_left[:, :half], "tensor", right)
            two = lax.ppermute(from_right[:, half:], "tensor", left)
            total = total + product(one, here - n // 2)
            total = total + product(two, here - n // 2, half)
        total = total + jnp.concatenate(expand(shrunk, expand_table, adapter_ids))
        return total.astype(BF16).reshape(chats, span, -1)

    return local


INWARD = [(0, 1), (3, 2)]
OUTWARD = [(1, 0), (2, 3)]
ACROSS = [(1, 2), (2, 1)]
SWAP = INWARD + OUTWARD


def send(block, pairs):
    return lax.ppermute(block, "tensor", pairs)


def after(block, *earlier):
    return lax.optimization_barrier((block,) + earlier)[0]


def line(inputs, base_weight, shrink_table, expand_table, adapter_ids):
    chats, span, width = inputs.shape
    rows = chats * span
    here = lax.axis_index("tensor")
    is_end = (here == 0) | (here == 3)
    far_mid = jnp.where(here < 2, 2, 1)
    far_end = jnp.where(here < 2, 3, 0)
    own = inputs.reshape(rows, width)
    half, last = width // 2, width // 8

    def product(block, owner, first=0):
        part = lax.dynamic_slice_in_dim(base_weight, owner * width + first, block.shape[1], axis=0)
        return jnp.dot(block, part, preferred_element_type=F32)

    mate = send(own, SWAP)
    partial = shrink(inputs, shrink_table, adapter_ids)
    mid = [send(after(own, partial)[:, :half], ACROSS)]
    mate_partial = send(partial, INWARD)
    total = product(own, here)
    mid.append(send(after(own, total)[:, half:], ACROSS))

    mid_out = [send(after(mid[0], total), OUTWARD)]
    mate, mate_partial = lax.optimization_barrier((mate, mate_partial, mid[0], total))[:2]
    both = send(jnp.stack([partial, mate_partial]), ACROSS)
    first = mate[:, :half]
    end = [send(first, ACROSS)]
    end.append(send(after(mate, end[0])[:, half:], ACROSS))
    mid_out.append(send(after(mid[1], first), OUTWARD))
    total = total + product(mate, here ^ 1)

    end[0], both = lax.optimization_barrier((end[0], both, total))[:2]
    end_out = [send(end[0], OUTWARD)]
    shrunk = (
        partial.astype(F32) + mate_partial.astype(F32) + both[0].astype(F32) + both[1].astype(F32)
    ).astype(BF16)
    shrunk = jnp.where(is_end, send(shrunk, OUTWARD), shrunk)
    total = total + product(jnp.where(is_end, mid_out[0], mid[0]), far_mid)

    late = after(end[1], total)
    begin = (after(far_end, late) + 1) * width - last
    last_rows = lax.dynamic_slice_in_dim(base_weight, begin, last, axis=0)
    late, last_rows = lax.optimization_barrier((late, last_rows))
    shrunk = after(shrunk, late)
    end_out += [send(late[:, : half - last], OUTWARD), send(late[:, half - last :], OUTWARD)]
    total = total + product(jnp.where(is_end, mid_out[1], mid[1]), far_mid, half)
    total = total + jnp.concatenate(expand(shrunk, expand_table, adapter_ids))
    total = total + product(jnp.where(is_end, end_out[0], end[0]), far_end)
    block = jnp.where(is_end, after(end_out[1], total), late[:, : half - last])
    total = total + product(block, far_end, half)
    block = jnp.where(is_end, after(end_out[2], total), late[:, half - last :])
    total = total + jnp.dot(block, last_rows, preferred_element_type=F32)
    return total.astype(BF16).reshape(chats, span, -1)


def solution(mesh):
    n = mesh.shape["tensor"]
    return jax.shard_map(
        line if n == 4 else ring(n),
        mesh=mesh,
        in_specs=(
            P(("groups", "dp"), "seq", "tensor"),
            P(None, "tensor"),
            P("groups", "tensor", None),
            P("groups", None, "tensor"),
            P(("groups", "dp")),
        ),
        out_specs=P(("groups", "dp"), "seq", "tensor"),
        check_vma=False,
    )
```

```python
import jax
import jax.numpy as jnp
from jax import lax
from jax.sharding import PartitionSpec as P

F32, BF16 = jnp.float32, jnp.bfloat16


def shrink(inputs, shrink_table, adapter_ids):
    return jnp.concatenate(
        [
            jnp.dot(inputs[c], shrink_table[adapter_ids[c]], preferred_element_type=F32).astype(BF16)
            for c in range(inputs.shape[0])
        ]
    )


def expand(shrunk, expand_table, adapter_ids):
    chats = adapter_ids.shape[0]
    parts = shrunk.reshape(chats, -1, shrunk.shape[-1])
    return [
        jnp.dot(parts[c], expand_table[adapter_ids[c]], preferred_element_type=F32)
        for c in range(chats)
    ]


def ring(n):
    right = [(i, (i + 1) % n) for i in range(n)]
    left = [(i, (i - 1) % n) for i in range(n)]

    def local(inputs, base_weight, shrink_table, expand_table, adapter_ids):
        chats, span, width = inputs.shape
        here = lax.axis_index("tensor")
        own = inputs.reshape(chats * span, width)

        def product(block, owner, first=0):
            rows = lax.dynamic_slice_in_dim(
                base_weight, lax.rem(owner + 2 * n, n) * width + first, block.shape[1], axis=0
            )
            return jnp.dot(block, rows, preferred_element_type=F32)

        shrunk = lax.psum(shrink(inputs, shrink_table, adapter_ids), "tensor")
        total = product(own, here)
        from_left = from_right = own
        for step in range(1, (n - 1) // 2 + 1):
            from_left = lax.ppermute(from_left, "tensor", right)
            from_right = lax.ppermute(from_right, "tensor", left)
            total = total + product(from_left, here - step)
            total = total + product(from_right, here + step)
        if n > 1 and n % 2 == 0:
            half = width // 2
            one = lax.ppermute(from_left[:, :half], "tensor", right)
            two = lax.ppermute(from_right[:, half:], "tensor", left)
            total = total + product(one, here - n // 2)
            total = total + product(two, here - n // 2, half)
        total = total + jnp.concatenate(expand(shrunk, expand_table, adapter_ids))
        return total.astype(BF16).reshape(chats, span, -1)

    return local


INWARD = [(0, 1), (3, 2)]
OUTWARD = [(1, 0), (2, 3)]
ACROSS = [(1, 2), (2, 1)]
SWAP = INWARD + OUTWARD


def send(block, pairs):
    return lax.ppermute(block, "tensor", pairs)


def after(block, *earlier):
    return lax.optimization_barrier((block,) + earlier)[0]


def line(inputs, base_weight, shrink_table, expand_table, adapter_ids):
    chats, span, width = inputs.shape
    rows = chats * span
    here = lax.axis_index("tensor")
    is_end = (here == 0) | (here == 3)
    far_mid = jnp.where(here < 2, 2, 1)
    far_end = jnp.where(here < 2, 3, 0)
    own = inputs.reshape(rows, width)
    half, last = width // 2, width // 8

    def product(block, owner, first=0):
        part = lax.dynamic_slice_in_dim(base_weight, owner * width + first, block.shape[1], axis=0)
        return jnp.dot(block, part, preferred_element_type=F32)

    mate = send(own, SWAP)
    mid = [send(own[:, :half], ACROSS)]
    partial = shrink(inputs, shrink_table, adapter_ids)
    mid.append(send(after(own, partial)[:, half:], ACROSS))
    mate_partial = send(partial, INWARD)
    total = product(own, here)

    mid_out = [send(after(mid[0], total), OUTWARD)]
    mate, mate_partial = lax.optimization_barrier((mate, mate_partial, mid[0], total))[:2]
    both = send(jnp.stack([partial, mate_partial]), ACROSS)
    first = mate[:, :half]
    end = [send(first, ACROSS)]
    end.append(send(after(mate, end[0])[:, half:], ACROSS))
    mid_out.append(send(after(mid[1], first), OUTWARD))
    total = total + product(mate, here ^ 1)

    end[0], both = lax.optimization_barrier((end[0], both, total))[:2]
    end_out = [send(end[0], OUTWARD)]
    shrunk = (
        partial.astype(F32) + mate_partial.astype(F32) + both[0].astype(F32) + both[1].astype(F32)
    ).astype(BF16)
    shrunk = jnp.where(is_end, send(shrunk, OUTWARD), shrunk)
    total = total + product(jnp.where(is_end, mid_out[0], mid[0]), far_mid)

    late = after(end[1], total)
    begin = (after(far_end, late) + 1) * width - last
    last_rows = lax.dynamic_slice_in_dim(base_weight, begin, last, axis=0)
    late, last_rows = lax.optimization_barrier((late, last_rows))
    shrunk = after(shrunk, late)
    end_out += [send(late[:, : half - last], OUTWARD), send(late[:, half - last :], OUTWARD)]
    total = total + product(jnp.where(is_end, mid_out[1], mid[1]), far_mid, half)
    total = total + jnp.concatenate(expand(shrunk, expand_table, adapter_ids))
    total = total + product(jnp.where(is_end, end_out[0], end[0]), far_end)
    total = total + product(late, far_end, half)
    total = total + product(after(end_out[1], total), far_end, half)
    total = total + jnp.dot(after(end_out[2], total), last_rows, preferred_element_type=F32)
    return total.astype(BF16).reshape(chats, span, -1)


def solution(mesh):
    n = mesh.shape["tensor"]
    return jax.shard_map(
        line if n == 4 else ring(n),
        mesh=mesh,
        in_specs=(
            P(("groups", "dp"), "seq", "tensor"),
            P(None, "tensor"),
            P("groups", "tensor", None),
            P("groups", None, "tensor"),
            P(("groups", "dp")),
        ),
        out_specs=P(("groups", "dp"), "seq", "tensor"),
        check_vma=False,
    )
```

```python
import jax
import jax.numpy as jnp
from jax import lax
from jax.sharding import PartitionSpec as P

F32, BF16 = jnp.float32, jnp.bfloat16


def shrink(inputs, shrink_table, adapter_ids):
    return jnp.concatenate(
        [
            jnp.dot(inputs[c], shrink_table[adapter_ids[c]], preferred_element_type=F32).astype(BF16)
            for c in range(inputs.shape[0])
        ]
    )


def expand(shrunk, expand_table, adapter_ids):
    chats = adapter_ids.shape[0]
    parts = shrunk.reshape(chats, -1, shrunk.shape[-1])
    return [
        jnp.dot(parts[c], expand_table[adapter_ids[c]], preferred_element_type=F32)
        for c in range(chats)
    ]


def ring(n):
    right = [(i, (i + 1) % n) for i in range(n)]
    left = [(i, (i - 1) % n) for i in range(n)]

    def local(inputs, base_weight, shrink_table, expand_table, adapter_ids):
        chats, span, width = inputs.shape
        here = lax.axis_index("tensor")
        own = inputs.reshape(chats * span, width)

        def product(block, owner, first=0):
            rows = lax.dynamic_slice_in_dim(
                base_weight, lax.rem(owner + 2 * n, n) * width + first, block.shape[1], axis=0
            )
            return jnp.dot(block, rows, preferred_element_type=F32)

        shrunk = lax.psum(shrink(inputs, shrink_table, adapter_ids), "tensor")
        total = product(own, here)
        from_left = from_right = own
        for step in range(1, (n - 1) // 2 + 1):
            from_left = lax.ppermute(from_left, "tensor", right)
            from_right = lax.ppermute(from_right, "tensor", left)
            total = total + product(from_left, here - step)
            total = total + product(from_right, here + step)
        if n > 1 and n % 2 == 0:
            half = width // 2
            one = lax.ppermute(from_left[:, :half], "tensor", right)
            two = lax.ppermute(from_right[:, half:], "tensor", left)
            total = total + product(one, here - n // 2)
            total = total + product(two, here - n // 2, half)
        total = total + jnp.concatenate(expand(shrunk, expand_table, adapter_ids))
        return total.astype(BF16).reshape(chats, span, -1)

    return local


INWARD = [(0, 1), (3, 2)]
OUTWARD = [(1, 0), (2, 3)]
ACROSS = [(1, 2), (2, 1)]
SWAP = INWARD + OUTWARD


def send(block, pairs):
    return lax.ppermute(block, "tensor", pairs)


def after(block, *earlier):
    return lax.optimization_barrier((block,) + earlier)[0]


def line(inputs, base_weight, shrink_table, expand_table, adapter_ids):
    chats, span, width = inputs.shape
    rows = chats * span
    here = lax.axis_index("tensor")
    is_end = (here == 0) | (here == 3)
    far_mid = jnp.where(here < 2, 2, 1)
    far_end = jnp.where(here < 2, 3, 0)
    own = inputs.reshape(rows, width)
    half, last = width // 2, width // 16 * 3

    def product(block, owner, first=0):
        part = lax.dynamic_slice_in_dim(base_weight, owner * width + first, block.shape[1], axis=0)
        return jnp.dot(block, part, preferred_element_type=F32)

    mate = send(own, SWAP)
    mid = [send(own[:, :half], ACROSS)]
    partial = shrink(inputs, shrink_table, adapter_ids)
    mid.append(send(after(own, partial)[:, half:], ACROSS))
    mate_partial = send(partial, INWARD)
    total = product(own, here)

    mid_out = [send(after(mid[0], total), OUTWARD)]
    mate, mate_partial = lax.optimization_barrier((mate, mate_partial, mid[0], total))[:2]
    both = send(jnp.stack([partial, mate_partial]), ACROSS)
    first = mate[:, :half]
    end = [send(first, ACROSS)]
    end.append(send(after(mate, end[0])[:, half:], ACROSS))
    mid_out.append(send(after(mid[1], first), OUTWARD))
    total = total + product(mate, here ^ 1)

    end[0], both = lax.optimization_barrier((end[0], both, total))[:2]
    end_out = [send(end[0], OUTWARD)]
    shrunk = (
        partial.astype(F32) + mate_partial.astype(F32) + both[0].astype(F32) + both[1].astype(F32)
    ).astype(BF16)
    shrunk = jnp.where(is_end, send(shrunk, OUTWARD), shrunk)
    total = total + product(jnp.where(is_end, mid_out[0], mid[0]), far_mid)

    late = after(end[1], total)
    begin = (after(far_end, late) + 1) * width - last
    last_rows = lax.dynamic_slice_in_dim(base_weight, begin, last, axis=0)
    late, last_rows = lax.optimization_barrier((late, last_rows))
    shrunk = after(shrunk, late)
    end_out += [send(late[:, : half - last], OUTWARD), send(late[:, half - last :], OUTWARD)]
    total = total + product(jnp.where(is_end, mid_out[1], mid[1]), far_mid, half)
    total = total + jnp.concatenate(expand(shrunk, expand_table, adapter_ids))
    total = total + product(jnp.where(is_end, end_out[0], end[0]), far_end)
    block = jnp.where(is_end, after(end_out[1], total), late[:, : half - last])
    total = total + product(block, far_end, half)
    block = jnp.where(is_end, after(end_out[2], total), late[:, half - last :])
    total = total + jnp.dot(block, last_rows, preferred_element_type=F32)
    return total.astype(BF16).reshape(chats, span, -1)


def solution(mesh):
    n = mesh.shape["tensor"]
    return jax.shard_map(
        line if n == 4 else ring(n),
        mesh=mesh,
        in_specs=(
            P(("groups", "dp"), "seq", "tensor"),
            P(None, "tensor"),
            P("groups", "tensor", None),
            P("groups", None, "tensor"),
            P(("groups", "dp")),
        ),
        out_specs=P(("groups", "dp"), "seq", "tensor"),
        check_vma=False,
    )
```

```python
import jax
import jax.numpy as jnp
from jax import lax
from jax.sharding import PartitionSpec as P

F32, BF16 = jnp.float32, jnp.bfloat16


def shrink(inputs, shrink_table, adapter_ids):
    return jnp.concatenate(
        [
            jnp.dot(inputs[c], shrink_table[adapter_ids[c]], preferred_element_type=F32).astype(BF16)
            for c in range(inputs.shape[0])
        ]
    )


def expand(shrunk, expand_table, adapter_ids):
    chats = adapter_ids.shape[0]
    parts = shrunk.reshape(chats, -1, shrunk.shape[-1])
    return [
        jnp.dot(parts[c], expand_table[adapter_ids[c]], preferred_element_type=F32)
        for c in range(chats)
    ]


def ring(n):
    right = [(i, (i + 1) % n) for i in range(n)]
    left = [(i, (i - 1) % n) for i in range(n)]

    def local(inputs, base_weight, shrink_table, expand_table, adapter_ids):
        chats, span, width = inputs.shape
        here = lax.axis_index("tensor")
        own = inputs.reshape(chats * span, width)

        def product(block, owner, first=0):
            rows = lax.dynamic_slice_in_dim(
                base_weight, lax.rem(owner + 2 * n, n) * width + first, block.shape[1], axis=0
            )
            return jnp.dot(block, rows, preferred_element_type=F32)

        shrunk = lax.psum(shrink(inputs, shrink_table, adapter_ids), "tensor")
        total = product(own, here)
        from_left = from_right = own
        for step in range(1, (n - 1) // 2 + 1):
            from_left = lax.ppermute(from_left, "tensor", right)
            from_right = lax.ppermute(from_right, "tensor", left)
            total = total + product(from_left, here - step)
            total = total + product(from_right, here + step)
        if n > 1 and n % 2 == 0:
            half = width // 2
            one = lax.ppermute(from_left[:, :half], "tensor", right)
            two = lax.ppermute(from_right[:, half:], "tensor", left)
            total = total + product(one, here - n // 2)
            total = total + product(two, here - n // 2, half)
        total = total + jnp.concatenate(expand(shrunk, expand_table, adapter_ids))
        return total.astype(BF16).reshape(chats, span, -1)

    return local


INWARD = [(0, 1), (3, 2)]
OUTWARD = [(1, 0), (2, 3)]
ACROSS = [(1, 2), (2, 1)]
SWAP = INWARD + OUTWARD


def send(block, pairs):
    return lax.ppermute(block, "tensor", pairs)


def after(block, *earlier):
    return lax.optimization_barrier((block,) + earlier)[0]


def line(inputs, base_weight, shrink_table, expand_table, adapter_ids):
    chats, span, width = inputs.shape
    rows = chats * span
    here = lax.axis_index("tensor")
    is_end = (here == 0) | (here == 3)
    far_mid = jnp.where(here < 2, 2, 1)
    far_end = jnp.where(here < 2, 3, 0)
    own = inputs.reshape(rows, width)
    half, last = width // 2, width // 8

    def product(block, owner, first=0):
        part = lax.dynamic_slice_in_dim(base_weight, owner * width + first, block.shape[1], axis=0)
        return jnp.dot(block, part, preferred_element_type=F32)

    mid = send(own, ACROSS)
    mate = send(own, SWAP)
    partial = shrink(inputs, shrink_table, adapter_ids)
    mate_partial = send(partial, INWARD)
    total = product(own, here)

    mid_out = send(after(mid, total), OUTWARD)
    mate, mate_partial = lax.optimization_barrier((mate, mate_partial, mid, total))[:2]
    both = send(jnp.stack([partial, mate_partial]), ACROSS)
    first = mate[:, :half]
    end = [send(first, ACROSS)]
    end.append(send(after(mate, end[0])[:, half:], ACROSS))
    total = total + product(mate, here ^ 1)

    end[0], both = lax.optimization_barrier((end[0], both, total))[:2]
    end_out = [send(end[0], OUTWARD)]
    shrunk = (
        partial.astype(F32) + mate_partial.astype(F32) + both[0].astype(F32) + both[1].astype(F32)
    ).astype(BF16)
    shrunk = jnp.where(is_end, send(shrunk, OUTWARD), shrunk)

    late = after(end[1], total)
    begin = (after(far_end, late) + 1) * width - last
    last_rows = lax.dynamic_slice_in_dim(base_weight, begin, last, axis=0)
    late, last_rows = lax.optimization_barrier((late, last_rows))
    mid_out, shrunk = lax.optimization_barrier((mid_out, shrunk, late))[:2]
    end_out += [send(late[:, : half - last], OUTWARD), send(late[:, half - last :], OUTWARD)]
    total = total + product(jnp.where(is_end, mid_out, mid), far_mid)
    total = total + jnp.concatenate(expand(shrunk, expand_table, adapter_ids))
    total = total + product(jnp.where(is_end, end_out[0], end[0]), far_end)
    block = jnp.where(is_end, after(end_out[1], total), late[:, : half - last])
    total = total + product(block, far_end, half)
    block = jnp.where(is_end, after(end_out[2], total), late[:, half - last :])
    total = total + jnp.dot(block, last_rows, preferred_element_type=F32)
    return total.astype(BF16).reshape(chats, span, -1)


def solution(mesh):
    n = mesh.shape["tensor"]
    return jax.shard_map(
        line if n == 4 else ring(n),
        mesh=mesh,
        in_specs=(
            P(("groups", "dp"), "seq", "tensor"),
            P(None, "tensor"),
            P("groups", "tensor", None),
            P("groups", None, "tensor"),
            P(("groups", "dp")),
        ),
        out_specs=P(("groups", "dp"), "seq", "tensor"),
        check_vma=False,
    )
```

```python
import jax
import jax.numpy as jnp
from jax import lax
from jax.sharding import PartitionSpec as P

F32, BF16 = jnp.float32, jnp.bfloat16


def shrink(inputs, shrink_table, adapter_ids):
    return jnp.concatenate(
        [
            jnp.dot(inputs[c], shrink_table[adapter_ids[c]], preferred_element_type=F32).astype(BF16)
            for c in range(inputs.shape[0])
        ]
    )


def expand(shrunk, expand_table, adapter_ids):
    chats = adapter_ids.shape[0]
    parts = shrunk.reshape(chats, -1, shrunk.shape[-1])
    return [
        jnp.dot(parts[c], expand_table[adapter_ids[c]], preferred_element_type=F32)
        for c in range(chats)
    ]


def ring(n):
    right = [(i, (i + 1) % n) for i in range(n)]
    left = [(i, (i - 1) % n) for i in range(n)]

    def local(inputs, base_weight, shrink_table, expand_table, adapter_ids):
        chats, span, width = inputs.shape
        here = lax.axis_index("tensor")
        own = inputs.reshape(chats * span, width)

        def product(block, owner, first=0):
            rows = lax.dynamic_slice_in_dim(
                base_weight, lax.rem(owner + 2 * n, n) * width + first, block.shape[1], axis=0
            )
            return jnp.dot(block, rows, preferred_element_type=F32)

        shrunk = lax.psum(shrink(inputs, shrink_table, adapter_ids), "tensor")
        total = product(own, here)
        from_left = from_right = own
        for step in range(1, (n - 1) // 2 + 1):
            from_left = lax.ppermute(from_left, "tensor", right)
            from_right = lax.ppermute(from_right, "tensor", left)
            total = total + product(from_left, here - step)
            total = total + product(from_right, here + step)
        if n > 1 and n % 2 == 0:
            half = width // 2
            one = lax.ppermute(from_left[:, :half], "tensor", right)
            two = lax.ppermute(from_right[:, half:], "tensor", left)
            total = total + product(one, here - n // 2)
            total = total + product(two, here - n // 2, half)
        total = total + jnp.concatenate(expand(shrunk, expand_table, adapter_ids))
        return total.astype(BF16).reshape(chats, span, -1)

    return local


INWARD = [(0, 1), (3, 2)]
OUTWARD = [(1, 0), (2, 3)]
ACROSS = [(1, 2), (2, 1)]
SWAP = INWARD + OUTWARD


def send(block, pairs):
    return lax.ppermute(block, "tensor", pairs)


def after(block, *earlier):
    return lax.optimization_barrier((block,) + earlier)[0]


def line(inputs, base_weight, shrink_table, expand_table, adapter_ids):
    chats, span, width = inputs.shape
    rows = chats * span
    here = lax.axis_index("tensor")
    is_end = (here == 0) | (here == 3)
    far_mid = jnp.where(here < 2, 2, 1)
    far_end = jnp.where(here < 2, 3, 0)
    own = inputs.reshape(rows, width)
    half, cut, last = width // 2, width // 16 * 7, width // 16 * 3

    def product(block, owner, first=0):
        part = lax.dynamic_slice_in_dim(base_weight, owner * width + first, block.shape[1], axis=0)
        return jnp.dot(block, part, preferred_element_type=F32)

    mate = send(own, SWAP)
    mid = [send(own[:, :half], ACROSS)]
    partial = shrink(inputs, shrink_table, adapter_ids)
    mid.append(send(after(own, partial)[:, half:], ACROSS))
    mate_partial = send(partial, INWARD)
    total = product(own, here)

    mid_out = [send(after(mid[0], total), OUTWARD)]
    mate, mate_partial = lax.optimization_barrier((mate, mate_partial, mid[0], total))[:2]
    both = send(jnp.stack([partial, mate_partial]), ACROSS)
    first = mate[:, :cut]
    end = [send(first, ACROSS)]
    end.append(send(after(mate, end[0])[:, cut:], ACROSS))
    mid_out.append(send(after(mid[1], first), OUTWARD))
    total = total + product(mate, here ^ 1)

    end[0], both = lax.optimization_barrier((end[0], both, total))[:2]
    end_out = [send(end[0], OUTWARD)]
    shrunk = (
        partial.astype(F32) + mate_partial.astype(F32) + both[0].astype(F32) + both[1].astype(F32)
    ).astype(BF16)
    shrunk = jnp.where(is_end, send(shrunk, OUTWARD), shrunk)
    total = total + product(jnp.where(is_end, mid_out[0], mid[0]), far_mid)

    late = after(end[1], total)
    begin = (after(far_end, late) + 1) * width - last
    last_rows = lax.dynamic_slice_in_dim(base_weight, begin, last, axis=0)
    late, last_rows = lax.optimization_barrier((late, last_rows))
    shrunk = after(shrunk, late)
    end_out += [send(late[:, :-last], OUTWARD), send(late[:, -last:], OUTWARD)]
    total = total + product(jnp.where(is_end, mid_out[1], mid[1]), far_mid, half)
    total = total + jnp.concatenate(expand(shrunk, expand_table, adapter_ids))
    total = total + product(jnp.where(is_end, end_out[0], end[0]), far_end)
    block = jnp.where(is_end, after(end_out[1], total), late[:, :-last])
    total = total + product(block, far_end, cut)
    block = jnp.where(is_end, after(end_out[2], total), late[:, -last:])
    total = total + jnp.dot(block, last_rows, preferred_element_type=F32)
    return total.astype(BF16).reshape(chats, span, -1)


def solution(mesh):
    n = mesh.shape["tensor"]
    return jax.shard_map(
        line if n == 4 else ring(n),
        mesh=mesh,
        in_specs=(
            P(("groups", "dp"), "seq", "tensor"),
            P(None, "tensor"),
            P("groups", "tensor", None),
            P("groups", None, "tensor"),
            P(("groups", "dp")),
        ),
        out_specs=P(("groups", "dp"), "seq", "tensor"),
        check_vma=False,
    )
```

```python
import jax
import jax.numpy as jnp
from jax import lax
from jax.sharding import PartitionSpec as P

F32, BF16 = jnp.float32, jnp.bfloat16


def shrink(inputs, shrink_table, adapter_ids):
    return jnp.concatenate(
        [
            jnp.dot(inputs[c], shrink_table[adapter_ids[c]], preferred_element_type=F32).astype(BF16)
            for c in range(inputs.shape[0])
        ]
    )


def expand(shrunk, expand_table, adapter_ids):
    chats = adapter_ids.shape[0]
    parts = shrunk.reshape(chats, -1, shrunk.shape[-1])
    return [
        jnp.dot(parts[c], expand_table[adapter_ids[c]], preferred_element_type=F32)
        for c in range(chats)
    ]


def ring(n):
    right = [(i, (i + 1) % n) for i in range(n)]
    left = [(i, (i - 1) % n) for i in range(n)]

    def local(inputs, base_weight, shrink_table, expand_table, adapter_ids):
        chats, span, width = inputs.shape
        here = lax.axis_index("tensor")
        own = inputs.reshape(chats * span, width)

        def product(block, owner, first=0):
            rows = lax.dynamic_slice_in_dim(
                base_weight, lax.rem(owner + 2 * n, n) * width + first, block.shape[1], axis=0
            )
            return jnp.dot(block, rows, preferred_element_type=F32)

        shrunk = lax.psum(shrink(inputs, shrink_table, adapter_ids), "tensor")
        total = product(own, here)
        from_left = from_right = own
        for step in range(1, (n - 1) // 2 + 1):
            from_left = lax.ppermute(from_left, "tensor", right)
            from_right = lax.ppermute(from_right, "tensor", left)
            total = total + product(from_left, here - step)
            total = total + product(from_right, here + step)
        if n > 1 and n % 2 == 0:
            half = width // 2
            one = lax.ppermute(from_left[:, :half], "tensor", right)
            two = lax.ppermute(from_right[:, half:], "tensor", left)
            total = total + product(one, here - n // 2)
            total = total + product(two, here - n // 2, half)
        total = total + jnp.concatenate(expand(shrunk, expand_table, adapter_ids))
        return total.astype(BF16).reshape(chats, span, -1)

    return local


INWARD = [(0, 1), (3, 2)]
OUTWARD = [(1, 0), (2, 3)]
ACROSS = [(1, 2), (2, 1)]
SWAP = INWARD + OUTWARD


def send(block, pairs):
    return lax.ppermute(block, "tensor", pairs)


def after(block, *earlier):
    return lax.optimization_barrier((block,) + earlier)[0]


def line(inputs, base_weight, shrink_table, expand_table, adapter_ids):
    chats, span, width = inputs.shape
    rows = chats * span
    here = lax.axis_index("tensor")
    is_end = (here == 0) | (here == 3)
    far_mid = jnp.where(here < 2, 2, 1)
    far_end = jnp.where(here < 2, 3, 0)
    own = inputs.reshape(rows, width)
    half, cut, last = width // 2, width // 16 * 7, width // 8

    def product(block, owner, first=0):
        part = lax.dynamic_slice_in_dim(base_weight, owner * width + first, block.shape[1], axis=0)
        return jnp.dot(block, part, preferred_element_type=F32)

    mate = send(own, SWAP)
    mid = [send(own[:, :half], ACROSS)]
    partial = shrink(inputs, shrink_table, adapter_ids)
    mid.append(send(after(own, partial)[:, half:], ACROSS))
    mate_partial = send(partial, INWARD)
    total = product(own, here)

    mid_out = [send(after(mid[0], total), OUTWARD)]
    mate, mate_partial = lax.optimization_barrier((mate, mate_partial, mid[0], total))[:2]
    both = send(jnp.stack([partial, mate_partial]), ACROSS)
    first = mate[:, :cut]
    end = [send(first, ACROSS)]
    end.append(send(after(mate, end[0])[:, cut:], ACROSS))
    mid_out.append(send(after(mid[1], first), OUTWARD))
    total = total + product(mate, here ^ 1)

    end[0], both = lax.optimization_barrier((end[0], both, total))[:2]
    end_out = [send(end[0], OUTWARD)]
    shrunk = (
        partial.astype(F32) + mate_partial.astype(F32) + both[0].astype(F32) + both[1].astype(F32)
    ).astype(BF16)
    shrunk = jnp.where(is_end, send(shrunk, OUTWARD), shrunk)
    total = total + product(jnp.where(is_end, mid_out[0], mid[0]), far_mid)

    late = after(end[1], total)
    begin = (after(far_end, late) + 1) * width - last
    last_rows = lax.dynamic_slice_in_dim(base_weight, begin, last, axis=0)
    next_rows = lax.dynamic_slice_in_dim(base_weight, begin + last - width + cut, width - cut - last)
    late, last_rows, next_rows = lax.optimization_barrier((late, last_rows, next_rows))
    shrunk = after(shrunk, late)
    end_out += [send(late[:, :-last], OUTWARD), send(late[:, -last:], OUTWARD)]
    total = total + product(jnp.where(is_end, mid_out[1], mid[1]), far_mid, half)
    total = total + jnp.concatenate(expand(shrunk, expand_table, adapter_ids))
    total = total + product(jnp.where(is_end, end_out[0], end[0]), far_end)
    block = jnp.where(is_end, after(end_out[1], total), late[:, :-last])
    total = total + jnp.dot(block, next_rows, preferred_element_type=F32)
    block = jnp.where(is_end, after(end_out[2], total), late[:, -last:])
    total = total + jnp.dot(block, last_rows, preferred_element_type=F32)
    return total.astype(BF16).reshape(chats, span, -1)


def solution(mesh):
    n = mesh.shape["tensor"]
    return jax.shard_map(
        line if n == 4 else ring(n),
        mesh=mesh,
        in_specs=(
            P(("groups", "dp"), "seq", "tensor"),
            P(None, "tensor"),
            P("groups", "tensor", None),
            P("groups", None, "tensor"),
            P(("groups", "dp")),
        ),
        out_specs=P(("groups", "dp"), "seq", "tensor"),
        check_vma=False,
    )
```

```python
import jax
import jax.numpy as jnp
from jax import lax
from jax.sharding import PartitionSpec as P

F32, BF16 = jnp.float32, jnp.bfloat16


def shrink(inputs, shrink_table, adapter_ids):
    return jnp.concatenate(
        [
            jnp.dot(inputs[c], shrink_table[adapter_ids[c]], preferred_element_type=F32).astype(BF16)
            for c in range(inputs.shape[0])
        ]
    )


def expand(shrunk, expand_table, adapter_ids):
    chats = adapter_ids.shape[0]
    parts = shrunk.reshape(chats, -1, shrunk.shape[-1])
    return [
        jnp.dot(parts[c], expand_table[adapter_ids[c]], preferred_element_type=F32)
        for c in range(chats)
    ]


def ring(n):
    right = [(i, (i + 1) % n) for i in range(n)]
    left = [(i, (i - 1) % n) for i in range(n)]

    def local(inputs, base_weight, shrink_table, expand_table, adapter_ids):
        chats, span, width = inputs.shape
        here = lax.axis_index("tensor")
        own = inputs.reshape(chats * span, width)

        def product(block, owner, first=0):
            rows = lax.dynamic_slice_in_dim(
                base_weight, lax.rem(owner + 2 * n, n) * width + first, block.shape[1], axis=0
            )
            return jnp.dot(block, rows, preferred_element_type=F32)

        shrunk = lax.psum(shrink(inputs, shrink_table, adapter_ids), "tensor")
        total = product(own, here)
        from_left = from_right = own
        for step in range(1, (n - 1) // 2 + 1):
            from_left = lax.ppermute(from_left, "tensor", right)
            from_right = lax.ppermute(from_right, "tensor", left)
            total = total + product(from_left, here - step)
            total = total + product(from_right, here + step)
        if n > 1 and n % 2 == 0:
            half = width // 2
            one = lax.ppermute(from_left[:, :half], "tensor", right)
            two = lax.ppermute(from_right[:, half:], "tensor", left)
            total = total + product(one, here - n // 2)
            total = total + product(two, here - n // 2, half)
        total = total + jnp.concatenate(expand(shrunk, expand_table, adapter_ids))
        return total.astype(BF16).reshape(chats, span, -1)

    return local


INWARD = [(0, 1), (3, 2)]
OUTWARD = [(1, 0), (2, 3)]
ACROSS = [(1, 2), (2, 1)]
SWAP = INWARD + OUTWARD


def send(block, pairs):
    return lax.ppermute(block, "tensor", pairs)


def after(block, *earlier):
    return lax.optimization_barrier((block,) + earlier)[0]


def line(inputs, base_weight, shrink_table, expand_table, adapter_ids):
    chats, span, width = inputs.shape
    rows = chats * span
    here = lax.axis_index("tensor")
    is_end = (here == 0) | (here == 3)
    far_mid = jnp.where(here < 2, 2, 1)
    far_end = jnp.where(here < 2, 3, 0)
    own = inputs.reshape(rows, width)
    half, cut, last = width // 2, width // 16 * 7, width // 16

    def product(block, owner, first=0):
        part = lax.dynamic_slice_in_dim(base_weight, owner * width + first, block.shape[1], axis=0)
        return jnp.dot(block, part, preferred_element_type=F32)

    mate = send(own, SWAP)
    mid = [send(own[:, :half], ACROSS)]
    partial = shrink(inputs, shrink_table, adapter_ids)
    mid.append(send(after(own, partial)[:, half:], ACROSS))
    mate_partial = send(partial, INWARD)
    total = product(own, here)

    mid_out = [send(after(mid[0], total), OUTWARD)]
    mate, mate_partial = lax.optimization_barrier((mate, mate_partial, mid[0], total))[:2]
    both = send(jnp.stack([partial, mate_partial]), ACROSS)
    first = mate[:, :cut]
    end = [send(first, ACROSS)]
    end.append(send(after(mate, end[0])[:, cut:], ACROSS))
    mid_out.append(send(after(mid[1], first), OUTWARD))
    total = total + product(mate, here ^ 1)

    end[0], both = lax.optimization_barrier((end[0], both, total))[:2]
    end_out = [send(end[0], OUTWARD)]
    shrunk = (
        partial.astype(F32) + mate_partial.astype(F32) + both[0].astype(F32) + both[1].astype(F32)
    ).astype(BF16)
    shrunk = jnp.where(is_end, send(shrunk, OUTWARD), shrunk)
    total = total + product(jnp.where(is_end, mid_out[0], mid[0]), far_mid)

    late = after(end[1], total)
    begin = (after(far_end, late) + 1) * width - last
    last_rows = lax.dynamic_slice_in_dim(base_weight, begin, last, axis=0)
    next_rows = lax.dynamic_slice_in_dim(base_weight, begin + last - width + cut, width - cut - last)
    late, last_rows, next_rows = lax.optimization_barrier((late, last_rows, next_rows))
    shrunk = after(shrunk, late)
    end_out += [send(late[:, :-last], OUTWARD), send(late[:, -last:], OUTWARD)]
    total = total + product(jnp.where(is_end, mid_out[1], mid[1]), far_mid, half)
    total = total + jnp.concatenate(expand(shrunk, expand_table, adapter_ids))
    total = total + product(jnp.where(is_end, end_out[0], end[0]), far_end)
    block = jnp.where(is_end, after(end_out[1], total), late[:, :-last])
    total = total + jnp.dot(block, next_rows, preferred_element_type=F32)
    block = jnp.where(is_end, after(end_out[2], total), late[:, -last:])
    total = total + jnp.dot(block, last_rows, preferred_element_type=F32)
    return total.astype(BF16).reshape(chats, span, -1)


def solution(mesh):
    n = mesh.shape["tensor"]
    return jax.shard_map(
        line if n == 4 else ring(n),
        mesh=mesh,
        in_specs=(
            P(("groups", "dp"), "seq", "tensor"),
            P(None, "tensor"),
            P("groups", "tensor", None),
            P("groups", None, "tensor"),
            P(("groups", "dp")),
        ),
        out_specs=P(("groups", "dp"), "seq", "tensor"),
        check_vma=False,
    )
```
